512 devices in a mesh: expert: 8 (over x, core), ffn: 64 (over y, z).
Axes of the slice: x: 4, y: 8, z: 8, core: 2. Of those that a mesh axis runs over, the one named last changes fastest.
Arguments:
- tokens: bfloat16 [64, 8, 4096], P('ffn', 'expert'), may hold values from -6 to 6
- routes: int32 [64, 8, 2], P('ffn'), may hold values from 0 to 7, all different within a row; in each aligned block of 8 rows (0 to 7, 8 to 15, ..., all dimensions but the last counted through in order) at most 4 rows name the same one
- routing_weight: float32 [64, 8, 2], P('ffn'), may hold values from 0.25 to 1
- gate_weight: bfloat16 [8, 12288, 4096], P('expert', 'ffn'), may hold values from -0.09375 to 0.09375
- up_weight: bfloat16 [8, 12288, 4096], P('expert', 'ffn'), may hold values from -0.09375 to 0.09375
- down_weight: bfloat16 [8, 12288, 4096], P('expert', 'ffn'), may hold values from -0.0546875 to 0.0546875
- adapter_input_maps: bfloat16 [4096, 128], P('ffn'), may hold values from -0.09375 to 0.09375
- adapter_output_maps: bfloat16 [8, 128, 12288], P('expert', None, 'ffn'), may hold values from -0.75 to 0.75
Outputs:
- mixed: bfloat16 [64, 8, 4096], P('ffn', 'expert')
The draws below stay inside these ranges and needn't reach their ends.
Inputs may be any that keep to these rules, and one draw needn't show every extreme that they name: `routes`: each token names 2 different experts. The 8 tokens of one index of ffn name each expert at most 4 times, and in every draw some expert exactly 4 times.
All inputs are finite; a program needn't handle non-finite values.
Results may differ from the reference program's by a relative error of at most 0.009.
Values may be sent and summed in bfloat16 or wider, within the bound.
No kernel may reach another device: no remote copies, remote signals or barrier semaphores. Data moves between devices by JAX's collectives and lax.ppermute only.
A program may use at most 64 MiB of HBM per device.

```python
import math
import jax
import jax.numpy as jnp
import numpy as np
from jax import lax

MODEL_WIDTH = 4096
HIDDEN_UNITS = 12288
EXPERT_COUNT = 8
ADAPTER_RANK = 64
TOP = 2
MOST = 4
TOKENS = 512
ROWS = 256
N_EXPERT = 8
N_FFN = 64


def block_levels(rng, extent, split, smallest, top_value):
    def one(axis_at, shards_of):
        heights = jax.random.uniform(jax.random.fold_in(jax.random.fold_in(rng, 6), axis_at), (shards_of,), jnp.float32, smallest / len(split), top_value / len(split))
        return jnp.repeat(jnp.exp(heights), extent[axis_at] // shards_of).reshape((-1,) + (1,) * (len(extent) - axis_at - 1))

    gain = one(*split[0])
    for cut in split[1:]:
        gain = gain * one(*cut)
    return gain


def shared_out(key, own, number, rows, number_of, top, reach, lean):
    order = jax.random.permutation(key, number_of)
    packed, common = portions_of(number_of, rows * top, reach, lean, True), portions_of(number_of, rows * top, reach, lean, False)
    places = jnp.arange(number_of)

    def named(lengths, offset_by):
        used = int((lengths > 0).sum())
        fixed = max(1, used // 4)
        passed = fixed + (places - fixed + offset_by * (used - fixed)) % max(1, number_of - fixed)
        return jnp.zeros((number_of,), jnp.int32).at[order[jnp.where(places < fixed, places, passed)]].set(jnp.asarray(lengths, jnp.int32))

    lengths = jnp.where(number % 4 == 0, named(packed, number // 4), named(common, number - number // 4 - 1))
    mixed = jax.random.permutation(jax.random.fold_in(own, 3), number_of)
    donor, sink = mixed[0:number_of // 2 * 2:2], mixed[1:number_of // 2 * 2:2]
    slack = jnp.minimum(lengths[donor] - 1, reach - lengths[sink]) // 2
    slack = jnp.where((donor == order[0]) | (sink == order[0]) | (lengths[sink] == 0), 0, jnp.maximum(slack, 0))
    passed = jax.random.randint(jax.random.fold_in(own, 4), (number_of // 2,), 0, 1 << 20) % (slack + 1)
    lengths = lengths.at[donor].add(-passed).at[sink].add(passed)
    items = jnp.searchsorted(jnp.cumsum(lengths), jnp.arange(rows * top), side="right").astype(jnp.int32)
    table = items.reshape(top, rows).T
    table = table[jax.random.permutation(jax.random.fold_in(own, 1), rows)]
    offset_by = jax.random.randint(jax.random.fold_in(own, 2), (rows, 1), 0, top)
    return jnp.take_along_axis(table, (jnp.arange(top)[None, :] + offset_by) % top, axis=1)


def portions_of(count, total, reach, skew, full):
    loads = [(1 << 20) // math.isqrt(grade ** skew) + 1 for grade in range(1, count + 1)]
    largest = reach if full else min(reach, max(-(-total // count), total * loads[0] // sum(loads)))
    least = 1 if total - largest >= count - 1 else 0
    holding, surplus = [largest] + [least] * (count - 1), total - largest - least * (count - 1)
    while surplus > 0:
        free = [i for i in range(1, count) if holding[i] < largest] or [i for i in range(1, count) if holding[i] < reach]
        pool, remaining = sum([loads[i] for i in free]), surplus
        for i in free:
            more = min(reach - holding[i], max(1, remaining * loads[i] // pool), surplus)
            holding[i] = holding[i] + more
            surplus = surplus - more
    return np.array(holding)


def centred(own_key, extent, scale, most, cuts=(), kind=jnp.bfloat16):
    result = jax.random.normal(own_key, extent, jnp.float32) * scale
    if len(cuts) > 0:
        result = block_levels(own_key, extent, cuts, -0.22, 0.18) * result
    return jnp.clip(result, min=-most, max=most).astype(kind)


def setup_inputs(seed: int = 0) -> dict:
    key_list = jax.random.split(jax.random.key(seed), 9)
    tokens = centred(key_list[0], (N_FFN, N_EXPERT, MODEL_WIDTH), 1.0, 6.0, ((0, 64), (1, 8)))
    routes_keys = jax.random.split(jax.random.fold_in(key_list[1], 1), N_FFN * N_EXPERT // N_EXPERT)
    routes_turns = jax.random.permutation(jax.random.fold_in(key_list[1], 3), N_FFN * N_EXPERT // N_EXPERT)
    routes = jax.vmap(lambda own, number: shared_out(jax.random.fold_in(key_list[1], 2), own, number, N_EXPERT, EXPERT_COUNT, TOP, MOST, 2))(routes_keys, routes_turns).reshape((N_FFN, N_EXPERT, TOP))
    routing_weight = jnp.clip(0.25 + 0.75 * jax.random.uniform(key_list[2], (N_FFN, N_EXPERT, TOP), jnp.float32) ** block_levels(key_list[2], (N_FFN, N_EXPERT, TOP), ((0, 64),), -0.2, 0.2), 0.25, 1.0)
    gate_weight = centred(key_list[3], (EXPERT_COUNT, HIDDEN_UNITS, MODEL_WIDTH), MODEL_WIDTH ** -0.5, 0.09375, ((0, 8), (1, 64)))
    up_weight = centred(key_list[4], (EXPERT_COUNT, HIDDEN_UNITS, MODEL_WIDTH), MODEL_WIDTH ** -0.5, 0.09375, ((0, 8), (1, 64)))
    down_weight = centred(key_list[5], (EXPERT_COUNT, HIDDEN_UNITS, MODEL_WIDTH), HIDDEN_UNITS ** -0.5, 0.0546875, ((0, 8), (1, 64)))
    adapter_input_maps = centred(key_list[6], (MODEL_WIDTH, 2 * ADAPTER_RANK), MODEL_WIDTH ** -0.5, 0.09375, ((0, 64),))
    adapter_output_maps = centred(key_list[7], (EXPERT_COUNT, 2 * ADAPTER_RANK, HIDDEN_UNITS), ADAPTER_RANK ** -0.5, 0.75, ((0, 8), (2, 64)))
    return {"tokens": tokens, "routes": routes, "routing_weight": routing_weight, "gate_weight": gate_weight, "up_weight": up_weight, "down_weight": down_weight, "adapter_input_maps": adapter_input_maps, "adapter_output_maps": adapter_output_maps}


adapter_scale = 0.5


def reference(tokens, routes, routing_weight, gate_weight, up_weight, down_weight, adapter_input_maps, adapter_output_maps):
    token_matrix = tokens.reshape(TOKENS, MODEL_WIDTH)
    route_ids = routes.reshape(TOKENS, TOP)
    weights = routing_weight.reshape(TOKENS, TOP)
    low_rank_values = jnp.dot(token_matrix, adapter_input_maps, preferred_element_type=jnp.float32).astype(jnp.bfloat16)

    def one_expert(total, expert_index):
        chosen = route_ids == expert_index
        hits = jnp.any(chosen, axis=1)
        count = jnp.sum(hits.astype(jnp.int32))
        picked = jnp.nonzero(hits, size=ROWS, fill_value=0)[0]
        live = (jnp.arange(ROWS) < count).astype(jnp.float32)
        rows_x = token_matrix[picked]
        row_low_rank = low_rank_values[picked]
        gate_values = jnp.dot(rows_x, gate_weight[expert_index].T, preferred_element_type=jnp.float32)
        gate_values = gate_values + adapter_scale * jnp.dot(row_low_rank[:, :ADAPTER_RANK], adapter_output_maps[expert_index, :ADAPTER_RANK], preferred_element_type=jnp.float32)
        up_values = jnp.dot(rows_x, up_weight[expert_index].T, preferred_element_type=jnp.float32)
        up_values = up_values + adapter_scale * jnp.dot(row_low_rank[:, ADAPTER_RANK:], adapter_output_maps[expert_index, ADAPTER_RANK:], preferred_element_type=jnp.float32)
        hidden = (jax.nn.silu(gate_values) * up_values).astype(jnp.bfloat16)
        output_rows = jnp.dot(hidden, down_weight[expert_index], preferred_element_type=jnp.float32).astype(jnp.bfloat16)
        output_rows = lax.optimization_barrier(output_rows).astype(jnp.float32)
        row_weight = jnp.sum(jnp.where(chosen[picked], weights[picked], 0.0), axis=1) * live
        total = total.at[picked].add(output_rows * row_weight[:, None])
        return total, None

    start = jnp.zeros((TOKENS, MODEL_WIDTH), jnp.float32)
    total, _ = lax.scan(one_expert, start, jnp.arange(EXPERT_COUNT, dtype=jnp.int32))
    return total.astype(jnp.bfloat16).reshape(N_FFN, N_EXPERT, MODEL_WIDTH)
```

```python
import jax
import jax.numpy as jnp
from jax import lax
from jax.sharding import Mesh, PartitionSpec as P

adapter_scale = 0.5
LINE = ("y", "z")


def contract(left, right):
    return lax.dot_general(
        left, right, (((1,), (1,)), ((), ())), preferred_element_type=jnp.float32
    )


def three_parts(value):
    high = lax.reduce_precision(value, 8, 7)
    rest = value - high
    middle = lax.reduce_precision(rest, 8, 7)
    return [high, middle, rest - middle]


def spread(block, axes, count):
    return lax.all_to_all(
        jnp.broadcast_to(block[None], (count,) + block.shape), axes, 0, 0, tiled=True
    )


def on_device(
    tokens,
    routes,
    routing_weight,
    gate_weight,
    up_weight,
    down_weight,
    adapter_input_maps,
    adapter_output_maps,
):
    bf16, f32 = jnp.bfloat16, jnp.float32
    chips, cores = lax.axis_size("x"), lax.axis_size("core")
    line = lax.axis_size("y") * lax.axis_size("z")
    core = lax.axis_index("core")
    expert = lax.axis_index("x") * cores + core
    experts = chips * cores
    width = tokens.shape[2]
    piece = width // 8
    rank = adapter_output_maps.shape[1] // 2

    own_routes = lax.dynamic_slice_in_dim(routes[0], expert, 1, 0)
    own_weights = lax.dynamic_slice_in_dim(routing_weight[0], expert, 1, 0)
    named = own_routes[0][None, :] == jnp.arange(experts, dtype=jnp.int32)[:, None]
    dense = jnp.sum(jnp.where(named, own_weights[0][None, :], 0.0), axis=1)
    parts = jnp.stack(three_parts(dense), axis=1).astype(bf16).reshape(1, 3 * experts)
    extra = jnp.pad(parts, ((0, 7), (0, 128 - 3 * experts)))
    maps_share = lax.dynamic_slice_in_dim(adapter_input_maps, expert * 8, 8, 0)
    block = jnp.concatenate([tokens.reshape(8, piece), maps_share, extra], axis=1)

    got = spread(block, LINE, line)
    rows = got[:, :, :piece].reshape(line, width)
    maps_tiles = (
        got[:, :, piece : piece + 128]
        .reshape(line // 8, 8, 8, 128)
        .transpose(0, 2, 1, 3)
        .reshape(line, 1024)
    )
    packed = jnp.concatenate([rows, maps_tiles, got[:, 0, piece + 128 :]], axis=1)
    own = spread(packed, "x", chips).reshape(chips * line, -1)
    swap = [(0, 1), (1, 0)]
    sibling = lax.ppermute(own, "core", swap)

    def tiles_of(both):
        return both[:, width : width + 1024].reshape(chips, line // 8, 8, 8, 128)

    first = jnp.where(core == 0, tiles_of(own), tiles_of(sibling))
    second = jnp.where(core == 0, tiles_of(sibling), tiles_of(own))
    maps = (
        jnp.stack([first, second], axis=1)
        .transpose(2, 4, 0, 1, 3, 5)
        .reshape(width, 128)
    )

    lane = jnp.arange(128, dtype=jnp.int32)[None, :] // 3

    def partial(both):
        x = both[:, :width]
        weight = jnp.sum(
            jnp.where(lane == expert, both[:, width + 1024 :].astype(f32), 0.0),
            axis=1,
            keepdims=True,
        )
        low = jnp.dot(x, maps, preferred_element_type=f32).astype(bf16)
        gate = contract(x, gate_weight[0])
        gate = gate + adapter_scale * jnp.dot(
            low[:, :rank], adapter_output_maps[0, :rank], preferred_element_type=f32
        )
        up = contract(x, up_weight[0])
        up = up + adapter_scale * jnp.dot(
            low[:, rank:], adapter_output_maps[0, rank:], preferred_element_type=f32
        )
        hidden = (jax.nn.silu(gate) * up).astype(bf16)
        return jnp.dot(hidden, down_weight[0], preferred_element_type=f32) * weight

    theirs = partial(sibling).astype(bf16)
    mine = partial(own)
    both = (mine + lax.ppermute(theirs, "core", swap).astype(f32)).astype(bf16)
    over_x = lax.all_to_all(both, "x", 0, 0, tiled=True).reshape(chips, line, width)
    column = jnp.sum(over_x.astype(f32), axis=0).astype(bf16)
    over_line = lax.all_to_all(column.reshape(line, 8, piece), LINE, 0, 0, tiled=True)
    mixed = jnp.sum(over_line.astype(f32), axis=0).astype(bf16)
    return mixed.reshape(1, 1, width)


def solution(mesh):
    grid = mesh.devices.shape
    side = 8 if grid[1] % 8 == 0 else 1
    fine = Mesh(
        mesh.devices.reshape(grid[0] // 2, 2, grid[1] // side, side),
        ("x", "core", "y", "z"),
    )
    wide = ("x", "core")
    in_specs = (
        P(LINE, wide, None),
        P(LINE, None, None),
        P(LINE, None, None),
        P(wide, LINE, None),
        P(wide, LINE, None),
        P(wide, LINE, None),
        P(LINE, None),
        P(wide, None, LINE),
    )
    return jax.shard_map(
        on_device, mesh=fine, in_specs=in_specs, out_specs=P(LINE, wide, None), check_vma=False
    )
```

```python
import functools

import jax
import jax.numpy as jnp
from jax import lax
from jax.experimental import pallas as pl
from jax.experimental.pallas import tpu as pltpu
from jax.sharding import Mesh, PartitionSpec as P

adapter_scale = 0.5
LINE = ("y", "z")
VMEM = pl.BlockSpec(memory_space=pltpu.VMEM)
SMEM = pl.BlockSpec(memory_space=pltpu.SMEM)
bf16, f32 = jnp.bfloat16, jnp.float32


def held(array):
    return pltpu.with_memory_space_constraint(array, pltpu.VMEM)


def on_core(kernel, outs, scratch=(), placed=0, arrays=0):
    return pl.pallas_call(
        kernel,
        in_specs=[SMEM] * placed + [VMEM] * arrays,
        out_specs=tuple(VMEM for _ in outs),
        out_shape=tuple(pltpu.VMEM(shape, kind) for shape, kind in outs),
        scratch_shapes=scratch,
        compiler_params=pltpu.CompilerParams(vmem_limit_bytes=16 << 20),
    )


def matmul(left, right, transposed):
    side = ((1,), (1 if transposed else 0,))
    return lax.dot_general(left, right, (side, ((), ())), preferred_element_type=f32)


def contract(left, right):
    return matmul(left, right, True)


def three_parts(value):
    high = lax.reduce_precision(value, 8, 7)
    rest = value - high
    middle = lax.reduce_precision(rest, 8, 7)
    return [high, middle, rest - middle]


def spread(block, axes, count):
    return lax.all_to_all(
        jnp.broadcast_to(block[None], (count,) + block.shape), axes, 0, 0, tiled=True
    )


def lay_maps(core, own_ref, sibling_ref, maps_ref):
    width = maps_ref.shape[0]
    line = width // 64
    chips = own_ref.shape[0] // line
    pairs = line // 16

    def step(i, carry):
        chip, pair = i // pairs, i % pairs
        rows = pl.ds(pl.multiple_of(chip * line + pair * 16, 16), 16)
        for b in range(8):
            lanes = slice(width + b * 128, width + (b + 1) * 128)
            one = own_ref[rows, lanes].astype(f32)
            other = sibling_ref[rows, lanes].astype(f32)
            even = jnp.where(core == 0, one, other)
            odd = jnp.where(core == 0, other, one)
            for half in range(2):
                at = 64 * (8 * (2 * pair + half) + b) + 16 * chip
                part = slice(8 * half, 8 * half + 8)
                maps_ref[pl.ds(pl.multiple_of(at, 16), 16), :] = jnp.concatenate(
                    [even[part], odd[part]], axis=0
                ).astype(bf16)
        return carry

    lax.fori_loop(0, chips * pairs, step, 0)


def hidden_of(expert, rows_ref, maps_ref, gate_ref, up_ref, out_maps_ref, total):
    width = maps_ref.shape[0]
    units = gate_ref.shape[0]
    rank = out_maps_ref.shape[0] // 2
    chunk = min(width, 1024)
    gate_at, up_at, low_at = slice(0, units), slice(256, 256 + units), slice(512, 640)

    def step(k, carry):
        lanes = pl.ds(pl.multiple_of(k * chunk, chunk), chunk)
        x = rows_ref[:, lanes]
        total[:, gate_at] += contract(x, gate_ref[:, lanes])
        total[:, up_at] += contract(x, up_ref[:, lanes])
        total[:, low_at] += matmul(x, maps_ref[lanes, :], False)
        return carry

    total[...] = jnp.zeros_like(total)
    lax.fori_loop(0, width // chunk, step, 0)
    low = total[:, low_at].astype(bf16)
    gate = total[:, gate_at] + adapter_scale * matmul(
        low[:, :rank], out_maps_ref[:rank, :], False
    )
    up = total[:, up_at] + adapter_scale * matmul(
        low[:, rank:], out_maps_ref[rank:, :], False
    )
    parts = rows_ref[:, width + 1024 :].astype(f32)
    lane = lax.broadcasted_iota(jnp.int32, parts.shape, 1)
    named = (lane >= 3 * expert) & (lane < 3 * expert + 3)
    weight = jnp.sum(jnp.where(named, parts, 0.0), axis=1, keepdims=True)
    return (jax.nn.silu(gate) * up * weight).astype(bf16)


def theirs_kernel(
    place, own_ref, sibling_ref, gate_ref, up_ref, down_ref, out_maps_ref, sum_ref, maps_ref, total
):
    lay_maps(place[0], own_ref, sibling_ref, maps_ref)
    hidden = hidden_of(
        place[1], sibling_ref, maps_ref, gate_ref, up_ref, out_maps_ref, total
    )
    wide = 512

    def step(n, carry):
        lanes = pl.ds(pl.multiple_of(n * wide, wide), wide)
        sum_ref[:, lanes] = matmul(hidden, down_ref[:, lanes], False).astype(bf16)
        return carry

    lax.fori_loop(0, sum_ref.shape[1] // wide, step, 0)


def hidden_kernel(
    place, own_ref, maps_ref, gate_ref, up_ref, out_maps_ref, hidden_ref, total
):
    hidden_ref[...] = hidden_of(
        place[1], own_ref, maps_ref, gate_ref, up_ref, out_maps_ref, total
    )


def add_kernel(hidden_ref, down_ref, came_ref, sum_ref):
    hidden = hidden_ref[...]
    wide = 512

    def step(n, carry):
        lanes = pl.ds(pl.multiple_of(n * wide, wide), wide)
        mine = matmul(hidden, down_ref[:, lanes], False)
        sum_ref[:, lanes] = (mine + came_ref[:, lanes].astype(f32)).astype(bf16)
        return carry

    lax.fori_loop(0, sum_ref.shape[1] // wide, step, 0)


def on_device(
    tokens,
    routes,
    routing_weight,
    gate_weight,
    up_weight,
    down_weight,
    adapter_input_maps,
    adapter_output_maps,
):
    chips, cores = lax.axis_size("x"), lax.axis_size("core")
    line = lax.axis_size("y") * lax.axis_size("z")
    core = lax.axis_index("core")
    expert = lax.axis_index("x") * cores + core
    experts = chips * cores
    width = tokens.shape[2]
    units = gate_weight.shape[1]
    piece = width // 8
    count = chips * line

    own_routes = lax.dynamic_slice_in_dim(routes[0], expert, 1, 0)
    own_weights = lax.dynamic_slice_in_dim(routing_weight[0], expert, 1, 0)
    named = own_routes[0][None, :] == jnp.arange(experts, dtype=jnp.int32)[:, None]
    dense = jnp.sum(jnp.where(named, own_weights[0][None, :], 0.0), axis=1)
    parts = jnp.stack(three_parts(dense), axis=1).astype(bf16).reshape(1, 3 * experts)
    extra = jnp.pad(parts, ((0, 7), (0, 128 - 3 * experts)))
    maps_share = lax.dynamic_slice_in_dim(adapter_input_maps, expert * 8, 8, 0)
    block = jnp.concatenate([tokens.reshape(8, piece), maps_share, extra], axis=1)

    got = spread(block, LINE, line)
    rows = got[:, :, :piece].reshape(line, width)
    maps_tiles = (
        got[:, :, piece : piece + 128]
        .reshape(line // 8, 8, 8, 128)
        .transpose(0, 2, 1, 3)
        .reshape(line, 1024)
    )
    packed = jnp.concatenate([rows, maps_tiles, got[:, 0, piece + 128 :]], axis=1)
    own = spread(packed, "x", chips).reshape(count, -1)
    swap = [(0, 1), (1, 0)]
    sibling = lax.ppermute(own, "core", swap)

    place = jnp.stack([core, expert]).astype(jnp.int32)
    own, sibling = held(own), held(sibling)
    gate, up, down = held(gate_weight[0]), held(up_weight[0]), held(down_weight[0])
    out_maps = held(adapter_output_maps[0])
    total = (pltpu.VMEM((count, 640), f32),)
    theirs, maps = on_core(
        theirs_kernel, (((count, width), bf16), ((width, 128), bf16)), total, 1, 6
    )(place, own, sibling, gate, up, down, out_maps)
    came = lax.ppermute(theirs, "core", swap)
    (hidden,) = on_core(hidden_kernel, (((count, units), bf16),), total, 1, 5)(
        place, own, held(maps), gate, up, out_maps
    )
    (both,) = on_core(add_kernel, (((count, width), bf16),), (), 0, 3)(
        held(hidden), down, held(came)
    )
    over_x = lax.all_to_all(both, "x", 0, 0, tiled=True).reshape(chips, line, width)
    column = jnp.sum(over_x.astype(f32), axis=0).astype(bf16)
    over_line = lax.all_to_all(column.reshape(line, 8, piece), LINE, 0, 0, tiled=True)
    mixed = jnp.sum(over_line.astype(f32), axis=0).astype(bf16)
    return mixed.reshape(1, 1, width)


def solution(mesh):
    grid = mesh.devices.shape
    side = 8 if grid[1] % 8 == 0 else 1
    fine = Mesh(
        mesh.devices.reshape(grid[0] // 2, 2, grid[1] // side, side),
        ("x", "core", "y", "z"),
    )
    wide = ("x", "core")
    in_specs = (
        P(LINE, wide, None),
        P(LINE, None, None),
        P(LINE, None, None),
        P(wide, LINE, None),
        P(wide, LINE, None),
        P(wide, LINE, None),
        P(LINE, None),
        P(wide, None, LINE),
    )
    return jax.shard_map(
        on_device, mesh=fine, in_specs=in_specs, out_specs=P(LINE, wide, None), check_vma=False
    )
```

```python
import functools

import jax
import jax.numpy as jnp
from jax import lax
from jax.experimental import pallas as pl
from jax.experimental.pallas import tpu as pltpu
from jax.sharding import Mesh, PartitionSpec as P

adapter_scale = 0.5
LINE = ("y_far", "y_near", "z_far", "z_near")
FAR = ("y_far", "z_far")
NEAR = ("x", "y_near", "z_near")
VMEM = pl.BlockSpec(memory_space=pltpu.VMEM)
HBM = pl.BlockSpec(memory_space=pltpu.HBM)
SMEM = pl.BlockSpec(memory_space=pltpu.SMEM)
bf16, f32 = jnp.bfloat16, jnp.float32


def held(array):
    return pltpu.with_memory_space_constraint(array, pltpu.VMEM)


def on_core(kernel, outs, scratch=(), placed=0, arrays=0, far=0):
    return pl.pallas_call(
        kernel,
        in_specs=[SMEM] * placed + [VMEM] * arrays + [HBM] * far,
        out_specs=tuple(VMEM for _ in outs),
        out_shape=tuple(pltpu.VMEM(shape, kind) for shape, kind in outs),
        scratch_shapes=scratch,
        compiler_params=pltpu.CompilerParams(vmem_limit_bytes=16 << 20),
    )


def matmul(left, right, transposed):
    side = ((1,), (1 if transposed else 0,))
    return lax.dot_general(left, right, (side, ((), ())), preferred_element_type=f32)


def contract(left, right):
    return matmul(left, right, True)


def three_parts(value):
    high = lax.reduce_precision(value, 8, 7)
    rest = value - high
    middle = lax.reduce_precision(rest, 8, 7)
    return [high, middle, rest - middle]


def spread(block, axes, count):
    return lax.all_to_all(
        jnp.broadcast_to(block[None], (count,) + block.shape), axes, 0, 0, tiled=True
    )


def lay_maps(core, far, own_ref, sibling_ref, maps_ref):
    width = maps_ref.shape[0]
    far_y, far_z = far
    count = far_y * far_z
    pairs = count // 16

    def step(i, carry):
        group, pair = i // pairs, i % pairs
        chip, near_y, near_z = group // 4, (group // 2) % 2, group % 2
        rows = pl.ds(pl.multiple_of(group * count + pair * 16, 16), 16)
        for b in range(8):
            lanes = slice(width + b * 128, width + (b + 1) * 128)
            one = own_ref[rows, lanes].astype(f32)
            other = sibling_ref[rows, lanes].astype(f32)
            even = jnp.where(core == 0, one, other)
            odd = jnp.where(core == 0, other, one)
            for half in range(2):
                place = 8 * (2 * pair + half) + b
                y, z = 2 * (place // far_z) + near_y, 2 * (place % far_z) + near_z
                at = 64 * (y * 2 * far_z + z) + 16 * chip
                part = slice(8 * half, 8 * half + 8)
                maps_ref[pl.ds(pl.multiple_of(at, 16), 16), :] = jnp.concatenate(
                    [even[part], odd[part]], axis=0
                ).astype(bf16)
        return carry

    lax.fori_loop(0, own_ref.shape[0] // count * pairs, step, 0)


def hidden_of(expert, rows_ref, maps_ref, gate_ref, up_ref, out_maps_ref, total):
    width = maps_ref.shape[0]
    units = gate_ref.shape[0]
    rank = out_maps_ref.shape[0] // 2
    chunk = min(width, 1024)
    gate_at, up_at, low_at = slice(0, units), slice(256, 256 + units), slice(512, 640)

    def step(k, carry):
        lanes = pl.ds(pl.multiple_of(k * chunk, chunk), chunk)
        x = rows_ref[:, lanes]
        total[:, gate_at] += contract(x, gate_ref[:, lanes])
        total[:, up_at] += contract(x, up_ref[:, lanes])
        total[:, low_at] += matmul(x, maps_ref[lanes, :], False)
        return carry

    total[...] = jnp.zeros_like(total)
    lax.fori_loop(0, width // chunk, step, 0)
    low = total[:, low_at].astype(bf16)
    gate = total[:, gate_at] + adapter_scale * matmul(
        low[:, :rank], out_maps_ref[:rank, :], False
    )
    up = total[:, up_at] + adapter_scale * matmul(
        low[:, rank:], out_maps_ref[rank:, :], False
    )
    parts = rows_ref[:, width + 1024 :].astype(f32)
    lane = lax.broadcasted_iota(jnp.int32, parts.shape, 1)
    named = (lane >= 3 * expert) & (lane < 3 * expert + 3)
    weight = jnp.sum(jnp.where(named, parts, 0.0), axis=1, keepdims=True)
    return (jax.nn.silu(gate) * up * weight).astype(bf16)


def theirs_kernel(
    far,
    place,
    own_ref,
    sibling_ref,
    out_maps_ref,
    gate_hbm,
    up_hbm,
    down_hbm,
    sum_ref,
    maps_ref,
    gate_ref,
    up_ref,
    down_ref,
    total,
    sems,
):
    copies = [
        pltpu.make_async_copy(source, target, sems.at[i])
        for i, (source, target) in enumerate(
            [(gate_hbm, gate_ref), (up_hbm, up_ref), (down_hbm, down_ref)]
        )
    ]
    for copy in copies:
        copy.start()
    lay_maps(place[0], far, own_ref, sibling_ref, maps_ref)
    for copy in copies:
        copy.wait()
    hidden = hidden_of(
        place[1], sibling_ref, maps_ref, gate_ref, up_ref, out_maps_ref, total
    )
    wide = 512

    def step(n, carry):
        lanes = pl.ds(pl.multiple_of(n * wide, wide), wide)
        sum_ref[:, lanes] = matmul(hidden, down_ref[:, lanes], False).astype(bf16)
        return carry

    lax.fori_loop(0, sum_ref.shape[1] // wide, step, 0)


def hidden_kernel(
    place, own_ref, maps_ref, gate_ref, up_ref, out_maps_ref, hidden_ref, total
):
    hidden_ref[...] = hidden_of(
        place[1], own_ref, maps_ref, gate_ref, up_ref, out_maps_ref, total
    )


def add_kernel(hidden_ref, down_ref, came_ref, sum_ref):
    hidden = hidden_ref[...]
    wide = 512

    def step(n, carry):
        lanes = pl.ds(pl.multiple_of(n * wide, wide), wide)
        mine = matmul(hidden, down_ref[:, lanes], False)
        sum_ref[:, lanes] = (mine + came_ref[:, lanes].astype(f32)).astype(bf16)
        return carry

    lax.fori_loop(0, sum_ref.shape[1] // wide, step, 0)


def on_device(
    tokens,
    routes,
    routing_weight,
    gate_weight,
    up_weight,
    down_weight,
    adapter_input_maps,
    adapter_output_maps,
):
    chips, cores = lax.axis_size("x"), lax.axis_size("core")
    far = (lax.axis_size("y_far"), lax.axis_size("z_far"))
    few = far[0] * far[1]
    groups = chips * 4
    core = lax.axis_index("core")
    expert = lax.axis_index("x") * cores + core
    experts = chips * cores
    width = tokens.shape[2]
    units = gate_weight.shape[1]
    piece = width // 8
    count = groups * few

    own_routes = lax.dynamic_slice_in_dim(routes[0], expert, 1, 0)
    own_weights = lax.dynamic_slice_in_dim(routing_weight[0], expert, 1, 0)
    named = own_routes[0][None, :] == jnp.arange(experts, dtype=jnp.int32)[:, None]
    dense = jnp.sum(jnp.where(named, own_weights[0][None, :], 0.0), axis=1)
    parts = jnp.stack(three_parts(dense), axis=1).astype(bf16).reshape(1, 3 * experts)
    extra = jnp.pad(parts, ((0, 7), (0, 128 - 3 * experts)))
    maps_share = lax.dynamic_slice_in_dim(adapter_input_maps, expert * 8, 8, 0)
    block = jnp.concatenate([tokens.reshape(8, piece), maps_share, extra], axis=1)

    got = spread(block, FAR, few)
    rows = got[:, :, :piece].reshape(few, width)
    maps_tiles = (
        got[:, :, piece : piece + 128]
        .reshape(few // 8, 8, 8, 128)
        .transpose(0, 2, 1, 3)
        .reshape(few, 1024)
    )
    packed = jnp.concatenate([rows, maps_tiles, got[:, 0, piece + 128 :]], axis=1)
    own = spread(packed, NEAR, groups).reshape(count, -1)
    swap = [(0, 1), (1, 0)]
    sibling = lax.ppermute(own, "core", swap)

    place = jnp.stack([core, expert]).astype(jnp.int32)
    own, sibling = held(own), held(sibling)
    weights = [
        pltpu.with_memory_space_constraint(w[0], pltpu.HBM)
        for w in (gate_weight, up_weight, down_weight)
    ]
    out_maps = held(adapter_output_maps[0])
    total = (pltpu.VMEM((count, 640), f32),)
    theirs, maps, gate, up, down = on_core(
        functools.partial(theirs_kernel, far),
        (((count, width), bf16), ((width, 128), bf16)) + (((units, width), bf16),) * 3,
        total + (pltpu.SemaphoreType.DMA((3,)),),
        1,
        3,
        3,
    )(place, own, sibling, out_maps, *weights)
    gate, up, down = held(gate), held(up), held(down)
    came = lax.ppermute(theirs, "core", swap)
    (hidden,) = on_core(hidden_kernel, (((count, units), bf16),), total, 1, 5)(
        place, own, held(maps), gate, up, out_maps
    )
    (both,) = on_core(add_kernel, (((count, width), bf16),), (), 0, 3)(
        held(hidden), down, held(came)
    )
    near = lax.all_to_all(both, NEAR, 0, 0, tiled=True).reshape(groups, few, width)
    column = jnp.sum(near.astype(f32), axis=0).astype(bf16)
    whole = lax.all_to_all(column.reshape(few, 8, piece), FAR, 0, 0, tiled=True)
    mixed = jnp.sum(whole.astype(f32), axis=0).astype(bf16)
    return mixed.reshape(1, 1, width)


def solution(mesh):
    expert, line = mesh.devices.shape
    fine = Mesh(
        mesh.devices.reshape(expert // 2, 2, line // 16, 2, 4, 2),
        ("x", "core") + LINE,
    )
    wide = ("x", "core")
    in_specs = (
        P(LINE, wide, None),
        P(LINE, None, None),
        P(LINE, None, None),
        P(wide, LINE, None),
        P(wide, LINE, None),
        P(wide, LINE, None),
        P(LINE, None),
        P(wide, None, LINE),
    )
    return jax.shard_map(
        on_device, mesh=fine, in_specs=in_specs, out_specs=P(LINE, wide, None), check_vma=False
    )
```

```python
import functools

import jax
import jax.numpy as jnp
from jax import lax
from jax.experimental import pallas as pl
from jax.experimental.pallas import tpu as pltpu
from jax.sharding import Mesh, PartitionSpec as P

adapter_scale = 0.5
LINE = ("y_far", "y_near", "z_far", "z_near")
FAR = ("y_far", "z_far")
NEAR = ("x", "y_near", "z_near")
VMEM = pl.BlockSpec(memory_space=pltpu.VMEM)
HBM = pl.BlockSpec(memory_space=pltpu.HBM)
SMEM = pl.BlockSpec(memory_space=pltpu.SMEM)
bf16, f32 = jnp.bfloat16, jnp.float32


def held(array):
    return pltpu.with_memory_space_constraint(array, pltpu.VMEM)


def on_core(kernel, outs, scratch=(), placed=0, arrays=0, far=0):
    return pl.pallas_call(
        kernel,
        in_specs=[SMEM] * placed + [VMEM] * arrays + [HBM] * far,
        out_specs=tuple(VMEM for _ in outs),
        out_shape=tuple(pltpu.VMEM(shape, kind) for shape, kind in outs),
        scratch_shapes=scratch,
        compiler_params=pltpu.CompilerParams(vmem_limit_bytes=16 << 20),
    )


def matmul(left, right, transposed):
    side = ((1,), (1 if transposed else 0,))
    return lax.dot_general(left, right, (side, ((), ())), preferred_element_type=f32)


def contract(left, right):
    return matmul(left, right, True)


def spread(block, axes, count):
    return lax.all_to_all(
        jnp.broadcast_to(block[None], (count,) + block.shape), axes, 0, 0, tiled=True
    )


def block_kernel(
    place, routes, weights, token_ref, maps_ref, block_ref, rows
):
    core, expert = place[0], place[1]
    piece = token_ref.shape[1] // 8
    token = token_ref[...].astype(f32)
    token = jnp.concatenate(
        [token[:, s * piece : (s + 1) * piece] for s in range(8)], axis=0
    )
    rows[...] = maps_ref[...].astype(f32)
    start = 32 * core + 8 * (expert // 2)
    share = rows[pl.ds(pl.multiple_of(start, 8), 8), :]
    lane = lax.broadcasted_iota(jnp.int32, (8, 128), 1)
    first = lax.broadcasted_iota(jnp.int32, (8, 128), 0) == 0
    extra = jnp.zeros((8, 128), f32)
    for use in range(routes.shape[0]):
        weight = jnp.full((8, 128), weights[use, expert], f32)
        high = weight.astype(bf16).astype(f32)
        rest = weight - high
        middle = rest.astype(bf16).astype(f32)
        at = jnp.where(first, lane - 3 * routes[use, expert], -1)
        extra = jnp.where(at == 0, high, extra)
        extra = jnp.where(at == 1, middle, extra)
        extra = jnp.where(at == 2, rest - middle, extra)
    block = jnp.concatenate([token, share, extra], axis=1).astype(bf16)
    block_ref[...] = jnp.broadcast_to(block[None], block_ref.shape)


def lay_half(core, far, rows_ref, put):
    far_y, far_z = far
    count = far_y * far_z
    pairs = count // 16
    width = 64 * 4 * count

    def step(i, carry):
        near, rest = i // (2 * pairs), i % (2 * pairs)
        two, pair = rest // pairs, rest % pairs
        near_y, near_z = near // 2, near % 2

        def rows_of(chip):
            return pl.ds(pl.multiple_of((chip * 4 + near) * count + pair * 16, 16), 16)

        for b in range(8):
            lanes = slice(width + b * 128, width + (b + 1) * 128)
            low = rows_ref[rows_of(2 * two), lanes].astype(f32)
            high = rows_ref[rows_of(2 * two + 1), lanes].astype(f32)
            for half in range(2):
                place = 8 * (2 * pair + half) + b
                y, z = 2 * (place // far_z) + near_y, 2 * (place % far_z) + near_z
                part = slice(8 * half, 8 * half + 8)
                put(
                    y * 2 * far_z + z,
                    two,
                    jnp.concatenate([low[part], high[part]], axis=0).astype(bf16),
                )
        return carry

    lax.fori_loop(0, 4 * 2 * pairs, step, 0)


def gate_and_up(rows_ref, gate_ref, up_ref, total):
    units, width = gate_ref.shape
    chunk = min(width, 1024)

    def step(k, carry):
        lanes = pl.ds(pl.multiple_of(k * chunk, chunk), chunk)
        x = rows_ref[:, lanes]
        total[:, :units] += contract(x, gate_ref[:, lanes])
        total[:, 256 : 256 + units] += contract(x, up_ref[:, lanes])
        return carry

    total[...] = jnp.zeros_like(total)
    lax.fori_loop(0, width // chunk, step, 0)


def hidden_of(expert, rows_ref, maps_ref, out_maps_ref, total, units):
    width = maps_ref.shape[0]
    rank = out_maps_ref.shape[0] // 2
    chunk = min(width, 1024)

    def step(k, low):
        at = pl.ds(pl.multiple_of(k * chunk, chunk), chunk)
        return low + matmul(rows_ref[:, at], maps_ref[at, :], False)

    low = lax.fori_loop(
        0, width // chunk, step, jnp.zeros((rows_ref.shape[0], 2 * rank), f32)
    ).astype(bf16)
    gate = total[:, :units] + adapter_scale * matmul(
        low[:, :rank], out_maps_ref[:rank, :], False
    )
    up = total[:, 256 : 256 + units] + adapter_scale * matmul(
        low[:, rank:], out_maps_ref[rank:, :], False
    )
    parts = rows_ref[:, width + 1024 :].astype(f32)
    lane = lax.broadcasted_iota(jnp.int32, parts.shape, 1)
    named = (lane >= 3 * expert) & (lane < 3 * expert + 3)
    weight = jnp.sum(jnp.where(named, parts, 0.0), axis=1, keepdims=True)
    return (jax.nn.silu(gate) * up * weight).astype(bf16)


def down_into(hidden, down_ref, out_ref):
    wide = 512

    def step(n, carry):
        lanes = pl.ds(pl.multiple_of(n * wide, wide), wide)
        out_ref[:, lanes] = matmul(hidden, down_ref[:, lanes], False).astype(
            out_ref.dtype
        )
        return carry

    lax.fori_loop(0, out_ref.shape[1] // wide, step, 0)


def ready_kernel(
    far,
    place,
    own_ref,
    gate_hbm,
    up_hbm,
    down_hbm,
    total,
    half_ref,
    gate_ref,
    up_ref,
    down_ref,
    sems,
):
    copies = [
        pltpu.make_async_copy(source, target, sems.at[i])
        for i, (source, target) in enumerate(
            [(gate_hbm, gate_ref), (up_hbm, up_ref), (down_hbm, down_ref)]
        )
    ]
    for copy in copies:
        copy.start()

    def put(line, two, rows):
        half_ref[pl.ds(pl.multiple_of(32 * line + 16 * two, 16), 16), :] = rows

    lay_half(place[0], far, own_ref, put)
    copies[0].wait()
    copies[1].wait()
    gate_and_up(own_ref, gate_ref, up_ref, total)
    copies[2].wait()


def theirs_kernel(
    far,
    place,
    half_ref,
    sibling_ref,
    out_maps_ref,
    gate_ref,
    up_ref,
    down_ref,
    sum_ref,
    maps_ref,
    total,
):
    core = place[0]

    def put(line, two, rows):
        at = 64 * line + 32 * (1 - core) + 16 * two
        maps_ref[pl.ds(pl.multiple_of(at, 16), 16), :] = rows

    def mine(line, carry):
        at = pl.ds(pl.multiple_of(64 * line + 32 * core, 32), 32)
        maps_ref[at, :] = half_ref[pl.ds(pl.multiple_of(32 * line, 32), 32), :]
        return carry

    lax.fori_loop(0, maps_ref.shape[0] // 64, mine, 0)
    lay_half(core, far, sibling_ref, put)
    gate_and_up(sibling_ref, gate_ref, up_ref, total)
    hidden = hidden_of(
        place[1], sibling_ref, maps_ref, out_maps_ref, total, gate_ref.shape[0]
    )
    down_into(hidden, down_ref, sum_ref)


def mine_kernel(place, own_ref, total, maps_ref, out_maps_ref, down_ref, sum_ref):
    hidden = hidden_of(
        place[1], own_ref, maps_ref, out_maps_ref, total, down_ref.shape[0]
    )
    down_into(hidden, down_ref, sum_ref)


def add_kernel(mine_ref, came_ref, sum_ref):
    def step(n, carry):
        rows = pl.ds(pl.multiple_of(n * 16, 16), 16)
        sum_ref[rows, :] = (mine_ref[rows, :] + came_ref[rows, :].astype(f32)).astype(
            bf16
        )
        return carry

    lax.fori_loop(0, sum_ref.shape[0] // 16, step, 0)


def on_device(
    tokens,
    routes,
    routing_weight,
    gate_weight,
    up_weight,
    down_weight,
    adapter_input_maps,
    adapter_output_maps,
):
    chips, cores = lax.axis_size("x"), lax.axis_size("core")
    far = (lax.axis_size("y_far"), lax.axis_size("z_far"))
    few = far[0] * far[1]
    groups = chips * 4
    core = lax.axis_index("core")
    expert = lax.axis_index("x") * cores + core
    width = tokens.shape[2]
    units = gate_weight.shape[1]
    piece = width // 8
    count = groups * few

    place = jnp.stack([core, expert]).astype(jnp.int32)
    (blocks,) = on_core(
        block_kernel,
        (((few, 8, piece + 256), bf16),),
        (pltpu.VMEM(adapter_input_maps.shape, f32),),
        3,
        2,
    )(place, routes[0].T, routing_weight[0].T, tokens[0], adapter_input_maps)
    got = lax.all_to_all(blocks, FAR, 0, 0, tiled=True)
    rows = got[:, :, :piece].reshape(few, width)
    maps_tiles = (
        got[:, :, piece : piece + 128]
        .reshape(few // 8, 8, 8, 128)
        .transpose(0, 2, 1, 3)
        .reshape(few, 1024)
    )
    packed = jnp.concatenate([rows, maps_tiles, got[:, 0, piece + 128 :]], axis=1)
    own = spread(packed, NEAR, groups).reshape(count, -1)
    swap = [(0, 1), (1, 0)]
    sibling = lax.ppermute(own, "core", swap)

    own, sibling = held(own), held(sibling)
    weights = [
        pltpu.with_memory_space_constraint(w[0], pltpu.HBM)
        for w in (gate_weight, up_weight, down_weight)
    ]
    out_maps = held(adapter_output_maps[0])
    total = ((count, 512), f32)
    sums, held_weight = ((count, width), bf16), ((units, width), bf16)
    base, half, gate, up, down = on_core(
        functools.partial(ready_kernel, far),
        (total, ((width // 2, 128), bf16)) + (held_weight,) * 3,
        (pltpu.SemaphoreType.DMA((3,)),),
        1,
        1,
        3,
    )(place, own, *weights)
    gate, up, down = held(gate), held(up), held(down)
    theirs, maps = on_core(
        functools.partial(theirs_kernel, far),
        (sums, ((width, 128), bf16)),
        (pltpu.VMEM(*total),),
        1,
        6,
    )(place, held(half), sibling, out_maps, gate, up, down)
    came = lax.ppermute(theirs, "core", swap)
    (mine,) = on_core(mine_kernel, (((count, width), f32),), (), 1, 5)(
        place, own, held(base), held(maps), out_maps, down
    )
    (both,) = on_core(add_kernel, (sums,), (), 0, 2)(held(mine), held(came))
    near = lax.all_to_all(both, NEAR, 0, 0, tiled=True).reshape(groups, few, width)
    column = jnp.sum(near.astype(f32), axis=0).astype(bf16)
    whole = lax.all_to_all(column.reshape(few, 8, piece), FAR, 0, 0, tiled=True)
    mixed = jnp.sum(whole.astype(f32), axis=0).astype(bf16)
    return mixed.reshape(1, 1, width)


def solution(mesh):
    expert, line = mesh.devices.shape
    fine = Mesh(
        mesh.devices.reshape(expert // 2, 2, line // 16, 2, 4, 2),
        ("x", "core") + LINE,
    )
    wide = ("x", "core")
    in_specs = (
        P(LINE, wide, None),
        P(LINE, None, None),
        P(LINE, None, None),
        P(wide, LINE, None),
        P(wide, LINE, None),
        P(wide, LINE, None),
        P(LINE, None),
        P(wide, None, LINE),
    )
    return jax.shard_map(
        on_device, mesh=fine, in_specs=in_specs, out_specs=P(LINE, wide, None), check_vma=False
    )
```

```python
import functools

import jax
import jax.numpy as jnp
from jax import lax
from jax.experimental import pallas as pl
from jax.experimental.pallas import tpu as pltpu
from jax.sharding import Mesh, PartitionSpec as P

adapter_scale = 0.5
LINE = ("y_far", "y_near", "z_far", "z_near")
FAR = ("y_far", "z_far")
NEAR = ("x", "y_near", "z_near")
VMEM = pl.BlockSpec(memory_space=pltpu.VMEM)
HBM = pl.BlockSpec(memory_space=pltpu.HBM)
SMEM = pl.BlockSpec(memory_space=pltpu.SMEM)
bf16, f32 = jnp.bfloat16, jnp.float32


def held(array):
    return pltpu.with_memory_space_constraint(array, pltpu.VMEM)


def far_held(array):
    return pltpu.with_memory_space_constraint(array, pltpu.HBM)


def on_core(kernel, outs, scratch=(), placed=0, arrays=0, far=0):
    return pl.pallas_call(
        kernel,
        in_specs=[SMEM] * placed + [VMEM] * arrays + [HBM] * far,
        out_specs=tuple(VMEM for _ in outs),
        out_shape=tuple(pltpu.VMEM(shape, kind) for shape, kind in outs),
        scratch_shapes=scratch,
        compiler_params=pltpu.CompilerParams(vmem_limit_bytes=16 << 20),
    )


def matmul(left, right, transposed):
    side = ((1,), (1 if transposed else 0,))
    return lax.dot_general(left, right, (side, ((), ())), preferred_element_type=f32)


def contract(left, right):
    return matmul(left, right, True)


def spread(block, axes, count):
    return lax.all_to_all(
        jnp.broadcast_to(block[None], (count,) + block.shape), axes, 0, 0, tiled=True
    )


def block_kernel(
    place,
    routes_hbm,
    weights_hbm,
    token_hbm,
    maps_hbm,
    block_ref,
    routes,
    weights,
    token_ref,
    maps_ref,
    rows,
    sems,
):
    copies = [
        pltpu.make_async_copy(source, target, sems.at[i])
        for i, (source, target) in enumerate(
            [
                (routes_hbm, routes),
                (weights_hbm, weights),
                (token_hbm, token_ref),
                (maps_hbm, maps_ref),
            ]
        )
    ]
    for copy in copies:
        copy.start()
    for copy in copies:
        copy.wait()
    core, expert = place[0], place[1]
    piece = token_ref.shape[1] // 8
    token = token_ref[...].astype(f32)
    token = jnp.concatenate(
        [token[:, s * piece : (s + 1) * piece] for s in range(8)], axis=0
    )
    rows[...] = maps_ref[...].astype(f32)
    start = 32 * core + 8 * (expert // 2)
    share = rows[pl.ds(pl.multiple_of(start, 8), 8), :]
    lane = lax.broadcasted_iota(jnp.int32, (8, 128), 1)
    first = lax.broadcasted_iota(jnp.int32, (8, 128), 0) == 0
    extra = jnp.zeros((8, 128), f32)
    for use in range(routes.shape[0]):
        weight = jnp.full((8, 128), weights[use, expert], f32)
        high = weight.astype(bf16).astype(f32)
        rest = weight - high
        middle = rest.astype(bf16).astype(f32)
        at = jnp.where(first, lane - 3 * routes[use, expert], -1)
        extra = jnp.where(at == 0, high, extra)
        extra = jnp.where(at == 1, middle, extra)
        extra = jnp.where(at == 2, rest - middle, extra)
    block = jnp.concatenate([token, share, extra], axis=1).astype(bf16)
    block_ref[...] = jnp.broadcast_to(block[None], block_ref.shape)


def lay_half(far, rows_ref, put, i):
    far_y, far_z = far
    count = far_y * far_z
    pairs = count // 16
    width = 64 * 4 * count
    near, two = i // 2, i % 2
    near_y, near_z = near // 2, near % 2
    for pair in range(pairs):

        def rows_of(chip):
            return pl.ds(pl.multiple_of((chip * 4 + near) * count + pair * 16, 16), 16)

        for b in range(8):
            lanes = slice(width + b * 128, width + (b + 1) * 128)
            low = rows_ref[rows_of(2 * two), lanes].astype(f32)
            high = rows_ref[rows_of(2 * two + 1), lanes].astype(f32)
            for half in range(2):
                place = 8 * (2 * pair + half) + b
                y, z = 2 * (place // far_z) + near_y, 2 * (place % far_z) + near_z
                part = slice(8 * half, 8 * half + 8)
                put(
                    y * 2 * far_z + z,
                    two,
                    jnp.concatenate([low[part], high[part]], axis=0).astype(bf16),
                )


def gate_and_up(rows_ref, gate_ref, up_ref, total, beside):
    units, width = gate_ref.shape
    chunk = width // 4

    def step(k, carry):
        lanes = pl.ds(pl.multiple_of(k * chunk, chunk), chunk)
        x = rows_ref[:, lanes]
        beside(2 * k)
        total[:, :units] += contract(x, gate_ref[:, lanes])
        beside(2 * k + 1)
        total[:, 256 : 256 + units] += contract(x, up_ref[:, lanes])
        return carry

    total[...] = jnp.zeros_like(total)
    lax.fori_loop(0, 4, step, 0)


def hidden_of(expert, rows_ref, maps_ref, out_maps_ref, total, units):
    width = maps_ref.shape[0]
    rank = out_maps_ref.shape[0] // 2
    chunk = min(width, 1024)

    def step(k, low):
        at = pl.ds(pl.multiple_of(k * chunk, chunk), chunk)
        return low + matmul(rows_ref[:, at], maps_ref[at, :], False)

    low = lax.fori_loop(
        0, width // chunk, step, jnp.zeros((rows_ref.shape[0], 2 * rank), f32)
    ).astype(bf16)
    gate = total[:, :units] + adapter_scale * matmul(
        low[:, :rank], out_maps_ref[:rank, :], False
    )
    up = total[:, 256 : 256 + units] + adapter_scale * matmul(
        low[:, rank:], out_maps_ref[rank:, :], False
    )
    parts = rows_ref[:, width + 1024 :].astype(f32)
    lane = lax.broadcasted_iota(jnp.int32, parts.shape, 1)
    named = (lane >= 3 * expert) & (lane < 3 * expert + 3)
    weight = jnp.sum(jnp.where(named, parts, 0.0), axis=1, keepdims=True)
    return (jax.nn.silu(gate) * up * weight).astype(bf16)


def down_into(hidden, down_ref, out_ref):
    wide = 512

    def step(n, carry):
        lanes = pl.ds(pl.multiple_of(n * wide, wide), wide)
        out_ref[:, lanes] = matmul(hidden, down_ref[:, lanes], False).astype(
            out_ref.dtype
        )
        return carry

    lax.fori_loop(0, out_ref.shape[1] // wide, step, 0)


def ready_kernel(
    far,
    place,
    own_ref,
    gate_hbm,
    up_hbm,
    down_hbm,
    total,
    half_ref,
    gate_ref,
    up_ref,
    down_ref,
    sems,
):
    copies = [
        pltpu.make_async_copy(source, target, sems.at[i])
        for i, (source, target) in enumerate(
            [(gate_hbm, gate_ref), (up_hbm, up_ref), (down_hbm, down_ref)]
        )
    ]
    for copy in copies:
        copy.start()

    def put(line, two, rows):
        half_ref[pl.ds(pl.multiple_of(32 * line + 16 * two, 16), 16), :] = rows

    copies[0].wait()
    copies[1].wait()
    gate_and_up(
        own_ref, gate_ref, up_ref, total, functools.partial(lay_half, far, own_ref, put)
    )
    copies[2].wait()


def theirs_kernel(
    far,
    place,
    half_ref,
    sibling_ref,
    out_maps_ref,
    gate_ref,
    up_ref,
    down_ref,
    sum_ref,
    maps_ref,
    total,
):
    core = place[0]

    def put(line, two, rows):
        at = 64 * line + 32 * (1 - core) + 16 * two
        maps_ref[pl.ds(pl.multiple_of(at, 16), 16), :] = rows

    def mine(line, carry):
        at = pl.ds(pl.multiple_of(64 * line + 32 * core, 32), 32)
        maps_ref[at, :] = half_ref[pl.ds(pl.multiple_of(32 * line, 32), 32), :]
        return carry

    lax.fori_loop(0, maps_ref.shape[0] // 64, mine, 0)
    gate_and_up(
        sibling_ref,
        gate_ref,
        up_ref,
        total,
        functools.partial(lay_half, far, sibling_ref, put),
    )
    hidden = hidden_of(
        place[1], sibling_ref, maps_ref, out_maps_ref, total, gate_ref.shape[0]
    )
    down_into(hidden, down_ref, sum_ref)


def mine_kernel(place, own_ref, total, maps_ref, out_maps_ref, down_ref, sum_ref):
    hidden = hidden_of(
        place[1], own_ref, maps_ref, out_maps_ref, total, down_ref.shape[0]
    )
    down_into(hidden, down_ref, sum_ref)


def add_kernel(mine_ref, came_ref, sum_ref):
    def step(n, carry):
        rows = pl.ds(pl.multiple_of(n * 16, 16), 16)
        sum_ref[rows, :] = (mine_ref[rows, :] + came_ref[rows, :].astype(f32)).astype(
            bf16
        )
        return carry

    lax.fori_loop(0, sum_ref.shape[0] // 16, step, 0)


def on_device(
    tokens,
    routes,
    routing_weight,
    gate_weight,
    up_weight,
    down_weight,
    adapter_input_maps,
    adapter_output_maps,
):
    chips, cores = lax.axis_size("x"), lax.axis_size("core")
    far = (lax.axis_size("y_far"), lax.axis_size("z_far"))
    few = far[0] * far[1]
    groups = chips * 4
    core = lax.axis_index("core")
    expert = lax.axis_index("x") * cores + core
    width = tokens.shape[2]
    units = gate_weight.shape[1]
    piece = width // 8
    count = groups * few

    place = jnp.stack([core, expert]).astype(jnp.int32)
    (blocks,) = on_core(
        block_kernel,
        (((few, 8, piece + 256), bf16),),
        (
            pltpu.SMEM(routes.shape[:0:-1], jnp.int32),
            pltpu.SMEM(routes.shape[:0:-1], f32),
            pltpu.VMEM((1, width), bf16),
            pltpu.VMEM(adapter_input_maps.shape, bf16),
            pltpu.VMEM(adapter_input_maps.shape, f32),
            pltpu.SemaphoreType.DMA((4,)),
        ),
        1,
        0,
        4,
    )(
        place,
        far_held(routes[0].T),
        far_held(routing_weight[0].T),
        far_held(tokens[0]),
        far_held(adapter_input_maps),
    )
    got = lax.all_to_all(blocks, FAR, 0, 0, tiled=True)
    rows = got[:, :, :piece].reshape(few, width)
    maps_tiles = (
        got[:, :, piece : piece + 128]
        .reshape(few // 8, 8, 8, 128)
        .transpose(0, 2, 1, 3)
        .reshape(few, 1024)
    )
    packed = jnp.concatenate([rows, maps_tiles, got[:, 0, piece + 128 :]], axis=1)
    own = spread(packed, NEAR, groups).reshape(count, -1)
    swap = [(0, 1), (1, 0)]
    sibling = lax.ppermute(own, "core", swap)

    own, sibling = held(own), held(sibling)
    weights = [far_held(w[0]) for w in (gate_weight, up_weight, down_weight)]
    out_maps = held(adapter_output_maps[0])
    total = ((count, 512), f32)
    sums, held_weight = ((count, width), bf16), ((units, width), bf16)
    base, half, gate, up, down = on_core(
        functools.partial(ready_kernel, far),
        (total, ((width // 2, 128), bf16)) + (held_weight,) * 3,
        (pltpu.SemaphoreType.DMA((3,)),),
        1,
        1,
        3,
    )(place, own, *weights)
    gate, up, down = held(gate), held(up), held(down)
    theirs, maps = on_core(
        functools.partial(theirs_kernel, far),
        (sums, ((width, 128), bf16)),
        (pltpu.VMEM(*total),),
        1,
        6,
    )(place, held(half), sibling, out_maps, gate, up, down)
    came = lax.ppermute(theirs, "core", swap)
    (mine,) = on_core(mine_kernel, (((count, width), f32),), (), 1, 5)(
        place, own, held(base), held(maps), out_maps, down
    )
    (both,) = on_core(add_kernel, (sums,), (), 0, 2)(held(mine), held(came))
    near = lax.all_to_all(both, NEAR, 0, 0, tiled=True).reshape(groups, few, width)
    column = jnp.sum(near.astype(f32), axis=0).astype(bf16)
    whole = lax.all_to_all(column.reshape(few, 8, piece), FAR, 0, 0, tiled=True)
    mixed = jnp.sum(whole.astype(f32), axis=0).astype(bf16)
    return mixed.reshape(1, 1, width)


def solution(mesh):
    expert, line = mesh.devices.shape
    fine = Mesh(
        mesh.devices.reshape(expert // 2, 2, line // 16, 2, 4, 2),
        ("x", "core") + LINE,
    )
    wide = ("x", "core")
    in_specs = (
        P(LINE, wide, None),
        P(LINE, None, None),
        P(LINE, None, None),
        P(wide, LINE, None),
        P(wide, LINE, None),
        P(wide, LINE, None),
        P(LINE, None),
        P(wide, None, LINE),
    )
    return jax.shard_map(
        on_device, mesh=fine, in_specs=in_specs, out_specs=P(LINE, wide, None), check_vma=False
    )
```

```python
import functools

import jax
import jax.numpy as jnp
from jax import lax
from jax.experimental import pallas as pl
from jax.experimental.pallas import tpu as pltpu
from jax.sharding import Mesh, PartitionSpec as P

adapter_scale = 0.5
LINE = ("y_far", "y_near", "z_far", "z_near")
FAR = ("y_far", "z_far")
NEAR = ("x", "y_near", "z_near")
VMEM = pl.BlockSpec(memory_space=pltpu.VMEM)
HBM = pl.BlockSpec(memory_space=pltpu.HBM)
SMEM = pl.BlockSpec(memory_space=pltpu.SMEM)
bf16, f32 = jnp.bfloat16, jnp.float32


def held(array):
    return pltpu.with_memory_space_constraint(array, pltpu.VMEM)


def far_held(array):
    return pltpu.with_memory_space_constraint(array, pltpu.HBM)


def on_core(kernel, outs, scratch=(), placed=0, arrays=0, far=0):
    return pl.pallas_call(
        kernel,
        in_specs=[SMEM] * placed + [VMEM] * arrays + [HBM] * far,
        out_specs=tuple(VMEM for _ in outs),
        out_shape=tuple(pltpu.VMEM(shape, kind) for shape, kind in outs),
        scratch_shapes=scratch,
        compiler_params=pltpu.CompilerParams(vmem_limit_bytes=20 << 20),
    )


def matmul(left, right, transposed):
    side = ((1,), (1 if transposed else 0,))
    return lax.dot_general(left, right, (side, ((), ())), preferred_element_type=f32)


def contract(left, right):
    return matmul(left, right, True)


def spread(block, axes, count):
    return lax.all_to_all(
        jnp.broadcast_to(block[None], (count,) + block.shape), axes, 0, 0, tiled=True
    )


def block_kernel(
    place,
    routes_hbm,
    weights_hbm,
    token_hbm,
    maps_hbm,
    block_ref,
    routes,
    weights,
    token_ref,
    maps_ref,
    rows,
    sems,
):
    copies = [
        pltpu.make_async_copy(source, target, sems.at[i])
        for i, (source, target) in enumerate(
            [
                (routes_hbm, routes),
                (weights_hbm, weights),
                (token_hbm, token_ref),
                (maps_hbm, maps_ref),
            ]
        )
    ]
    for copy in copies:
        copy.start()
    for copy in copies:
        copy.wait()
    core, expert = place[0], place[1]
    piece = token_ref.shape[1] // 8
    token = token_ref[...].astype(f32)
    token = jnp.concatenate(
        [token[:, s * piece : (s + 1) * piece] for s in range(8)], axis=0
    )
    rows[...] = maps_ref[...].astype(f32)
    start = 32 * core + 8 * (expert // 2)
    share = rows[pl.ds(pl.multiple_of(start, 8), 8), :]
    lane = lax.broadcasted_iota(jnp.int32, (8, 128), 1)
    first = lax.broadcasted_iota(jnp.int32, (8, 128), 0) == 0
    extra = jnp.zeros((8, 128), f32)
    for use in range(routes.shape[0]):
        weight = jnp.full((8, 128), weights[use, expert], f32)
        high = weight.astype(bf16).astype(f32)
        rest = weight - high
        middle = rest.astype(bf16).astype(f32)
        at = jnp.where(first, lane - 3 * routes[use, expert], -1)
        extra = jnp.where(at == 0, high, extra)
        extra = jnp.where(at == 1, middle, extra)
        extra = jnp.where(at == 2, rest - middle, extra)
    block = jnp.concatenate([token, share, extra], axis=1).astype(bf16)
    block_ref[...] = jnp.broadcast_to(block[None], block_ref.shape)


def lay_half(far, rows_ref, put, i):
    far_y, far_z = far
    count = far_y * far_z
    pairs = count // 16
    width = 64 * 4 * count
    near, two = i // 2, i % 2
    near_y, near_z = near // 2, near % 2
    for pair in range(pairs):

        def rows_of(chip):
            return pl.ds((chip * 4 + near) * count + pair * 16, 16)

        for b in range(8):
            lanes = slice(width + b * 128, width + (b + 1) * 128)
            low = rows_ref[rows_of(2 * two), lanes].astype(f32)
            high = rows_ref[rows_of(2 * two + 1), lanes].astype(f32)
            for half in range(2):
                place = 8 * (2 * pair + half) + b
                y, z = 2 * (place // far_z) + near_y, 2 * (place % far_z) + near_z
                part = slice(8 * half, 8 * half + 8)
                put(
                    y * 2 * far_z + z,
                    two,
                    jnp.concatenate([low[part], high[part]], axis=0).astype(bf16),
                )


def gate_and_up(rows_ref, gate_ref, up_ref, total):
    units, width = gate_ref.shape
    total[:, :units] = contract(rows_ref[:, :width], gate_ref[...])
    total[:, 256 : 256 + units] = contract(rows_ref[:, :width], up_ref[...])


def hidden_of(expert, rows_ref, maps_ref, out_maps_ref, total, units):
    width = maps_ref.shape[0]
    rank = out_maps_ref.shape[0] // 2
    low = matmul(rows_ref[:, :width], maps_ref[...], False).astype(bf16)
    gate = total[:, :units] + adapter_scale * matmul(
        low[:, :rank], out_maps_ref[:rank, :], False
    )
    up = total[:, 256 : 256 + units] + adapter_scale * matmul(
        low[:, rank:], out_maps_ref[rank:, :], False
    )
    parts = rows_ref[:, width + 1024 :].astype(f32)
    lane = lax.broadcasted_iota(jnp.int32, parts.shape, 1)
    named = (lane >= 3 * expert) & (lane < 3 * expert + 3)
    weight = jnp.sum(jnp.where(named, parts, 0.0), axis=1, keepdims=True)
    return (jax.nn.silu(gate) * up * weight).astype(bf16)


def down_into(hidden, down_ref, out_ref):
    out_ref[...] = matmul(hidden, down_ref[...], False).astype(out_ref.dtype)


def ready_kernel(
    far,
    place,
    own_ref,
    gate_hbm,
    up_hbm,
    down_hbm,
    total,
    half_ref,
    gate_ref,
    up_ref,
    down_ref,
    sems,
):
    copies = [
        pltpu.make_async_copy(source, target, sems.at[i])
        for i, (source, target) in enumerate(
            [(gate_hbm, gate_ref), (up_hbm, up_ref), (down_hbm, down_ref)]
        )
    ]
    for copy in copies:
        copy.start()

    def put(line, two, rows):
        half_ref[pl.ds(32 * line + 16 * two, 16), :] = rows

    for i in range(8):
        lay_half(far, own_ref, put, i)
    copies[0].wait()
    copies[1].wait()
    gate_and_up(own_ref, gate_ref, up_ref, total)
    copies[2].wait()


def theirs_kernel(
    far,
    place,
    half_ref,
    sibling_ref,
    out_maps_ref,
    gate_ref,
    up_ref,
    down_ref,
    sum_ref,
    maps_ref,
    total,
):
    core = place[0]

    def put(line, two, rows):
        at = 64 * line + 32 * (1 - core) + 16 * two
        maps_ref[pl.ds(pl.multiple_of(at, 16), 16), :] = rows

    def mine(line, carry):
        at = pl.ds(pl.multiple_of(64 * line + 32 * core, 32), 32)
        maps_ref[at, :] = half_ref[pl.ds(pl.multiple_of(32 * line, 32), 32), :]
        return carry

    lax.fori_loop(0, maps_ref.shape[0] // 64, mine, 0)
    for i in range(8):
        lay_half(far, sibling_ref, put, i)
    gate_and_up(sibling_ref, gate_ref, up_ref, total)
    hidden = hidden_of(
        place[1], sibling_ref, maps_ref, out_maps_ref, total, gate_ref.shape[0]
    )
    down_into(hidden, down_ref, sum_ref)


def mine_kernel(place, own_ref, total, maps_ref, out_maps_ref, down_ref, sum_ref):
    hidden = hidden_of(
        place[1], own_ref, maps_ref, out_maps_ref, total, down_ref.shape[0]
    )
    down_into(hidden, down_ref, sum_ref)


def add_kernel(mine_ref, came_ref, sum_ref):
    def step(n, carry):
        rows = pl.ds(pl.multiple_of(n * 16, 16), 16)
        sum_ref[rows, :] = (mine_ref[rows, :] + came_ref[rows, :].astype(f32)).astype(
            bf16
        )
        return carry

    lax.fori_loop(0, sum_ref.shape[0] // 16, step, 0)


def on_device(
    tokens,
    routes,
    routing_weight,
    gate_weight,
    up_weight,
    down_weight,
    adapter_input_maps,
    adapter_output_maps,
):
    chips, cores = lax.axis_size("x"), lax.axis_size("core")
    far = (lax.axis_size("y_far"), lax.axis_size("z_far"))
    few = far[0] * far[1]
    groups = chips * 4
    core = lax.axis_index("core")
    expert = lax.axis_index("x") * cores + core
    width = tokens.shape[2]
    units = gate_weight.shape[1]
    piece = width // 8
    count = groups * few

    place = jnp.stack([core, expert]).astype(jnp.int32)
    (blocks,) = on_core(
        block_kernel,
        (((few, 8, piece + 256), bf16),),
        (
            pltpu.SMEM(routes.shape[:0:-1], jnp.int32),
            pltpu.SMEM(routes.shape[:0:-1], f32),
            pltpu.VMEM((1, width), bf16),
            pltpu.VMEM(adapter_input_maps.shape, bf16),
            pltpu.VMEM(adapter_input_maps.shape, f32),
            pltpu.SemaphoreType.DMA((4,)),
        ),
        1,
        0,
        4,
    )(
        place,
        far_held(routes[0].T),
        far_held(routing_weight[0].T),
        far_held(tokens[0]),
        far_held(adapter_input_maps),
    )
    got = lax.all_to_all(blocks, FAR, 0, 0, tiled=True)
    rows = got[:, :, :piece].reshape(few, width)
    maps_tiles = (
        got[:, :, piece : piece + 128]
        .reshape(few // 8, 8, 8, 128)
        .transpose(0, 2, 1, 3)
        .reshape(few, 1024)
    )
    packed = jnp.concatenate([rows, maps_tiles, got[:, 0, piece + 128 :]], axis=1)
    own = spread(packed, NEAR, groups).reshape(count, -1)
    swap = [(0, 1), (1, 0)]
    sibling = lax.ppermute(own, "core", swap)

    own, sibling = held(own), held(sibling)
    weights = [far_held(w[0]) for w in (gate_weight, up_weight, down_weight)]
    out_maps = held(adapter_output_maps[0])
    total = ((count, 512), f32)
    sums, held_weight = ((count, width), bf16), ((units, width), bf16)
    base, half, gate, up, down = on_core(
        functools.partial(ready_kernel, far),
        (total, ((width // 2, 128), bf16)) + (held_weight,) * 3,
        (pltpu.SemaphoreType.DMA((3,)),),
        1,
        1,
        3,
    )(place, own, *weights)
    gate, up, down = held(gate), held(up), held(down)
    theirs, maps = on_core(
        functools.partial(theirs_kernel, far),
        (sums, ((width, 128), bf16)),
        (pltpu.VMEM(*total),),
        1,
        6,
    )(place, held(half), sibling, out_maps, gate, up, down)
    came = lax.ppermute(theirs, "core", swap)
    (mine,) = on_core(mine_kernel, (((count, width), f32),), (), 1, 5)(
        place, own, held(base), held(maps), out_maps, down
    )
    (both,) = on_core(add_kernel, (sums,), (), 0, 2)(held(mine), held(came))
    near = lax.all_to_all(both, NEAR, 0, 0, tiled=True).reshape(groups, few, width)
    column = jnp.sum(near.astype(f32), axis=0).astype(bf16)
    whole = lax.all_to_all(column.reshape(few, 8, piece), FAR, 0, 0, tiled=True)
    mixed = jnp.sum(whole.astype(f32), axis=0).astype(bf16)
    return mixed.reshape(1, 1, width)


def solution(mesh):
    expert, line = mesh.devices.shape
    fine = Mesh(
        mesh.devices.reshape(expert // 2, 2, line // 16, 2, 4, 2),
        ("x", "core") + LINE,
    )
    wide = ("x", "core")
    in_specs = (
        P(LINE, wide, None),
        P(LINE, None, None),
        P(LINE, None, None),
        P(wide, LINE, None),
        P(wide, LINE, None),
        P(wide, LINE, None),
        P(LINE, None),
        P(wide, None, LINE),
    )
    return jax.shard_map(
        on_device, mesh=fine, in_specs=in_specs, out_specs=P(LINE, wide, None), check_vma=False
    )
```

```python
import functools

import jax
import jax.numpy as jnp
from jax import lax
from jax.experimental import pallas as pl
from jax.experimental.pallas import tpu as pltpu
from jax.sharding import Mesh, PartitionSpec as P

adapter_scale = 0.5
LINE = ("y_far", "y_near", "z")
FAR = ("y_far", "z")
NEAR = ("x", "y_near")
VMEM = pl.BlockSpec(memory_space=pltpu.VMEM)
HBM = pl.BlockSpec(memory_space=pltpu.HBM)
SMEM = pl.BlockSpec(memory_space=pltpu.SMEM)
bf16, f32 = jnp.bfloat16, jnp.float32


def held(array):
    return pltpu.with_memory_space_constraint(array, pltpu.VMEM)


def far_held(array):
    return pltpu.with_memory_space_constraint(array, pltpu.HBM)


def on_core(kernel, outs, scratch=(), placed=0, arrays=0, far=0):
    return pl.pallas_call(
        kernel,
        in_specs=[SMEM] * placed + [VMEM] * arrays + [HBM] * far,
        out_specs=tuple(VMEM for _ in outs),
        out_shape=tuple(pltpu.VMEM(shape, kind) for shape, kind in outs),
        scratch_shapes=scratch,
        compiler_params=pltpu.CompilerParams(vmem_limit_bytes=20 << 20),
    )


def matmul(left, right, transposed):
    side = ((1,), (1 if transposed else 0,))
    return lax.dot_general(left, right, (side, ((), ())), preferred_element_type=f32)


def contract(left, right):
    return matmul(left, right, True)


def spread(block, axes, count):
    return lax.all_to_all(
        jnp.broadcast_to(block[None], (count,) + block.shape), axes, 0, 0, tiled=True
    )


def block_kernel(
    place,
    routes_hbm,
    weights_hbm,
    token_hbm,
    maps_hbm,
    block_ref,
    routes,
    weights,
    token_ref,
    maps_ref,
    rows,
    sems,
):
    copies = [
        pltpu.make_async_copy(source, target, sems.at[i])
        for i, (source, target) in enumerate(
            [
                (routes_hbm, routes),
                (weights_hbm, weights),
                (token_hbm, token_ref),
                (maps_hbm, maps_ref),
            ]
        )
    ]
    for copy in copies:
        copy.start()
    for copy in copies:
        copy.wait()
    core, expert = place[0], place[1]
    piece = token_ref.shape[1] // 8
    token = token_ref[...].astype(f32)
    token = jnp.concatenate(
        [token[:, s * piece : (s + 1) * piece] for s in range(8)], axis=0
    )
    rows[...] = maps_ref[...].astype(f32)
    start = 32 * core + 8 * (expert // 2)
    share = rows[pl.ds(pl.multiple_of(start, 8), 8), :]
    lane = lax.broadcasted_iota(jnp.int32, (8, 128), 1)
    first = lax.broadcasted_iota(jnp.int32, (8, 128), 0) == 0
    extra = jnp.zeros((8, 128), f32)
    for use in range(routes.shape[0]):
        weight = jnp.full((8, 128), weights[use, expert], f32)
        high = weight.astype(bf16).astype(f32)
        rest = weight - high
        middle = rest.astype(bf16).astype(f32)
        at = jnp.where(first, lane - 3 * routes[use, expert], -1)
        extra = jnp.where(at == 0, high, extra)
        extra = jnp.where(at == 1, middle, extra)
        extra = jnp.where(at == 2, rest - middle, extra)
    block = jnp.concatenate([token, share, extra], axis=1).astype(bf16)
    block_ref[...] = jnp.broadcast_to(block[None], block_ref.shape)


def lay_half(far, rows_ref, put):
    far_y, far_z = far
    count = far_y * far_z
    width = 64 * 2 * count
    for near in range(2):
        for two in range(2):
            for pair in range(count // 16):
                for b in range(8):
                    lanes = slice(width + b * 128, width + (b + 1) * 128)
                    low, high = [
                        rows_ref[
                            pl.ds((chip * 2 + near) * count + pair * 16, 16), lanes
                        ].astype(f32)
                        for chip in (2 * two, 2 * two + 1)
                    ]
                    for half in range(2):
                        place = 8 * (2 * pair + half) + b
                        y, z = 2 * (place // far_z) + near, place % far_z
                        part = slice(8 * half, 8 * half + 8)
                        rows = jnp.concatenate([low[part], high[part]], axis=0)
                        put(y * far_z + z, two, rows.astype(bf16))


def gate_and_up(rows_ref, gate_ref, up_ref, total):
    units, width = gate_ref.shape
    total[:, :units] = contract(rows_ref[:, :width], gate_ref[...])
    total[:, 256 : 256 + units] = contract(rows_ref[:, :width], up_ref[...])


def hidden_of(expert, rows_ref, maps_ref, out_maps_ref, total, units):
    width = maps_ref.shape[0]
    rank = out_maps_ref.shape[0] // 2
    low = matmul(rows_ref[:, :width], maps_ref[...], False).astype(bf16)
    gate = total[:, :units] + adapter_scale * matmul(
        low[:, :rank], out_maps_ref[:rank, :], False
    )
    up = total[:, 256 : 256 + units] + adapter_scale * matmul(
        low[:, rank:], out_maps_ref[rank:, :], False
    )
    parts = rows_ref[:, width + 1024 :].astype(f32)
    lane = lax.broadcasted_iota(jnp.int32, parts.shape, 1)
    named = (lane >= 3 * expert) & (lane < 3 * expert + 3)
    weight = jnp.sum(jnp.where(named, parts, 0.0), axis=1, keepdims=True)
    return (jax.nn.silu(gate) * up * weight).astype(bf16)


def down_into(hidden, down_ref, out_ref):
    out_ref[...] = matmul(hidden, down_ref[...], False).astype(out_ref.dtype)


def ready_kernel(
    far,
    place,
    own_ref,
    gate_hbm,
    up_hbm,
    down_hbm,
    total,
    half_ref,
    gate_ref,
    up_ref,
    down_ref,
    sems,
):
    copies = [
        pltpu.make_async_copy(source, target, sems.at[i])
        for i, (source, target) in enumerate(
            [(gate_hbm, gate_ref), (up_hbm, up_ref), (down_hbm, down_ref)]
        )
    ]
    for copy in copies:
        copy.start()

    def put(line, two, rows):
        half_ref[pl.ds(32 * line + 16 * two, 16), :] = rows

    lay_half(far, own_ref, put)
    copies[0].wait()
    copies[1].wait()
    gate_and_up(own_ref, gate_ref, up_ref, total)
    copies[2].wait()


def theirs_kernel(
    far,
    place,
    half_ref,
    sibling_ref,
    out_maps_ref,
    gate_ref,
    up_ref,
    down_ref,
    sum_ref,
    maps_ref,
    total,
):
    core = place[0]

    def put(line, two, rows):
        at = 64 * line + 32 * (1 - core) + 16 * two
        maps_ref[pl.ds(pl.multiple_of(at, 16), 16), :] = rows

    def mine(line, carry):
        at = pl.ds(pl.multiple_of(64 * line + 32 * core, 32), 32)
        maps_ref[at, :] = half_ref[pl.ds(pl.multiple_of(32 * line, 32), 32), :]
        return carry

    lax.fori_loop(0, maps_ref.shape[0] // 64, mine, 0)
    lay_half(far, sibling_ref, put)
    gate_and_up(sibling_ref, gate_ref, up_ref, total)
    hidden = hidden_of(
        place[1], sibling_ref, maps_ref, out_maps_ref, total, gate_ref.shape[0]
    )
    down_into(hidden, down_ref, sum_ref)


def mine_kernel(place, own_ref, total, maps_ref, out_maps_ref, down_ref, sum_ref):
    hidden = hidden_of(
        place[1], own_ref, maps_ref, out_maps_ref, total, down_ref.shape[0]
    )
    down_into(hidden, down_ref, sum_ref)


def add_kernel(mine_ref, came_ref, sum_ref):
    def step(n, carry):
        rows = pl.ds(pl.multiple_of(n * 16, 16), 16)
        sum_ref[rows, :] = (mine_ref[rows, :] + came_ref[rows, :].astype(f32)).astype(
            bf16
        )
        return carry

    lax.fori_loop(0, sum_ref.shape[0] // 16, step, 0)


def on_device(
    tokens,
    routes,
    routing_weight,
    gate_weight,
    up_weight,
    down_weight,
    adapter_input_maps,
    adapter_output_maps,
):
    chips, cores = lax.axis_size("x"), lax.axis_size("core")
    far = (lax.axis_size("y_far"), lax.axis_size("z"))
    few = far[0] * far[1]
    groups = chips * 2
    core = lax.axis_index("core")
    expert = lax.axis_index("x") * cores + core
    width = tokens.shape[2]
    units = gate_weight.shape[1]
    piece = width // 8
    count = groups * few

    place = jnp.stack([core, expert]).astype(jnp.int32)
    (blocks,) = on_core(
        block_kernel,
        (((few, 8, piece + 256), bf16),),
        (
            pltpu.SMEM(routes.shape[:0:-1], jnp.int32),
            pltpu.SMEM(routes.shape[:0:-1], f32),
            pltpu.VMEM((1, width), bf16),
            pltpu.VMEM(adapter_input_maps.shape, bf16),
            pltpu.VMEM(adapter_input_maps.shape, f32),
            pltpu.SemaphoreType.DMA((4,)),
        ),
        1,
        0,
        4,
    )(
        place,
        far_held(routes[0].T),
        far_held(routing_weight[0].T),
        far_held(tokens[0]),
        far_held(adapter_input_maps),
    )
    got = lax.all_to_all(blocks, FAR, 0, 0, tiled=True)
    rows = got[:, :, :piece].reshape(few, width)
    maps_tiles = (
        got[:, :, piece : piece + 128]
        .reshape(few // 8, 8, 8, 128)
        .transpose(0, 2, 1, 3)
        .reshape(few, 1024)
    )
    packed = jnp.concatenate([rows, maps_tiles, got[:, 0, piece + 128 :]], axis=1)
    own = spread(packed, NEAR, groups).reshape(count, -1)
    swap = [(0, 1), (1, 0)]
    sibling = lax.ppermute(own, "core", swap)

    own, sibling = held(own), held(sibling)
    weights = [far_held(w[0]) for w in (gate_weight, up_weight, down_weight)]
    out_maps = held(adapter_output_maps[0])
    total = ((count, 512), f32)
    sums, held_weight = ((count, width), bf16), ((units, width), bf16)
    base, half, gate, up, down = on_core(
        functools.partial(ready_kernel, far),
        (total, ((width // 2, 128), bf16)) + (held_weight,) * 3,
        (pltpu.SemaphoreType.DMA((3,)),),
        1,
        1,
        3,
    )(place, own, *weights)
    gate, up, down = held(gate), held(up), held(down)
    theirs, maps = on_core(
        functools.partial(theirs_kernel, far),
        (sums, ((width, 128), bf16)),
        (pltpu.VMEM(*total),),
        1,
        6,
    )(place, held(half), sibling, out_maps, gate, up, down)
    came = lax.ppermute(theirs, "core", swap)
    (mine,) = on_core(mine_kernel, (((count, width), f32),), (), 1, 5)(
        place, own, held(base), held(maps), out_maps, down
    )
    (both,) = on_core(add_kernel, (sums,), (), 0, 2)(held(mine), held(came))
    near = lax.all_to_all(both, NEAR, 0, 0, tiled=True).reshape(groups, few, width)
    column = jnp.sum(near.astype(f32), axis=0).astype(bf16)
    whole = lax.all_to_all(column.reshape(few, 8, piece), FAR, 0, 0, tiled=True)
    mixed = jnp.sum(whole.astype(f32), axis=0).astype(bf16)
    return mixed.reshape(1, 1, width)


def solution(mesh):
    expert, line = mesh.devices.shape
    fine = Mesh(
        mesh.devices.reshape(expert // 2, 2, line // 16, 2, 8),
        ("x", "core") + LINE,
    )
    wide = ("x", "core")
    in_specs = (
        P(LINE, wide, None),
        P(LINE, None, None),
        P(LINE, None, None),
        P(wide, LINE, None),
        P(wide, LINE, None),
        P(wide, LINE, None),
        P(LINE, None),
        P(wide, None, LINE),
    )
    return jax.shard_map(
        on_device, mesh=fine, in_specs=in_specs, out_specs=P(LINE, wide, None), check_vma=False
    )
```

```python
import functools

import jax
import jax.numpy as jnp
from jax import lax
from jax.experimental import pallas as pl
from jax.experimental.pallas import tpu as pltpu
from jax.sharding import Mesh, PartitionSpec as P

adapter_scale = 0.5
LINE = ("y_far", "y_near", "z_far", "z_near")
FAR = ("y_far", "z_far")
NEAR = ("x", "y_near", "z_near")
VMEM = pl.BlockSpec(memory_space=pltpu.VMEM)
HBM = pl.BlockSpec(memory_space=pltpu.HBM)
SMEM = pl.BlockSpec(memory_space=pltpu.SMEM)
bf16, f32 = jnp.bfloat16, jnp.float32


def held(array):
    return pltpu.with_memory_space_constraint(array, pltpu.VMEM)


def far_held(array):
    return pltpu.with_memory_space_constraint(array, pltpu.HBM)


def on_core(kernel, outs, scratch=(), placed=0, arrays=0, far=0):
    return pl.pallas_call(
        kernel,
        in_specs=[SMEM] * placed + [VMEM] * arrays + [HBM] * far,
        out_specs=tuple(VMEM for _ in outs),
        out_shape=tuple(pltpu.VMEM(shape, kind) for shape, kind in outs),
        scratch_shapes=scratch,
        compiler_params=pltpu.CompilerParams(vmem_limit_bytes=32 << 20),
    )


def matmul(left, right, transposed):
    side = ((1,), (1 if transposed else 0,))
    return lax.dot_general(left, right, (side, ((), ())), preferred_element_type=f32)


def contract(left, right):
    return matmul(left, right, True)


def spread(block, axes, count):
    return lax.all_to_all(
        jnp.broadcast_to(block[None], (count,) + block.shape), axes, 0, 0, tiled=True
    )


def block_kernel(
    place,
    routes_hbm,
    weights_hbm,
    token_hbm,
    maps_hbm,
    block_ref,
    routes,
    weights,
    token_ref,
    maps_ref,
    rows,
    sems,
):
    copies = [
        pltpu.make_async_copy(source, target, sems.at[i])
        for i, (source, target) in enumerate(
            [
                (routes_hbm, routes),
                (weights_hbm, weights),
                (token_hbm, token_ref),
                (maps_hbm, maps_ref),
            ]
        )
    ]
    for copy in copies:
        copy.start()
    for copy in copies:
        copy.wait()
    core, expert = place[0], place[1]
    piece = token_ref.shape[1] // 8
    token = token_ref[...].astype(f32)
    token = jnp.concatenate(
        [token[:, s * piece : (s + 1) * piece] for s in range(8)], axis=0
    )
    rows[...] = maps_ref[...].astype(f32)
    start = 32 * core + 8 * (expert // 2)
    share = rows[pl.ds(pl.multiple_of(start, 8), 8), :]
    lane = lax.broadcasted_iota(jnp.int32, (8, 128), 1)
    first = lax.broadcasted_iota(jnp.int32, (8, 128), 0) == 0
    extra = jnp.zeros((8, 128), f32)
    for use in range(routes.shape[0]):
        weight = jnp.full((8, 128), weights[use, expert], f32)
        high = weight.astype(bf16).astype(f32)
        rest = weight - high
        middle = rest.astype(bf16).astype(f32)
        at = jnp.where(first, lane - 3 * routes[use, expert], -1)
        extra = jnp.where(at == 0, high, extra)
        extra = jnp.where(at == 1, middle, extra)
        extra = jnp.where(at == 2, rest - middle, extra)
    block = jnp.concatenate([token, share, extra], axis=1).astype(bf16)
    block_ref[...] = jnp.broadcast_to(block[None], block_ref.shape)


def lay_half(far, rows_ref, start, put, i):
    far_y, far_z = far
    count = far_y * far_z
    pairs = count // 16
    near, two = i // 2, i % 2
    near_y, near_z = near // 2, near % 2
    for pair in range(pairs):

        def rows_of(chip):
            return pl.ds((chip * 4 + near) * count + pair * 16, 16)

        for b in range(8):
            lanes = slice(start + b * 128, start + (b + 1) * 128)
            low = rows_ref[rows_of(2 * two), lanes].astype(f32)
            high = rows_ref[rows_of(2 * two + 1), lanes].astype(f32)
            for half in range(2):
                place = 8 * (2 * pair + half) + b
                y, z = 2 * (place // far_z) + near_y, 2 * (place % far_z) + near_z
                part = slice(8 * half, 8 * half + 8)
                put(
                    y * 2 * far_z + z,
                    two,
                    jnp.concatenate([low[part], high[part]], axis=0).astype(bf16),
                )


def early_kernel(far, own_ref, gate_hbm, up_hbm, total, half_ref, gate_ref, up_ref, sems):
    width = gate_ref.shape[2]
    copies = [
        pltpu.make_async_copy(source.at[i], target.at[i], sems.at[2 * i + j])
        for i in range(2)
        for j, (source, target) in enumerate([(gate_hbm, gate_ref), (up_hbm, up_ref)])
    ]
    for copy in copies:
        copy.start()

    def put(line, two, rows):
        half_ref[pl.ds(32 * line + 16 * two, 16), :] = rows

    for i in range(8):
        lay_half(far, own_ref, width, put, i)
    for i in range(2):
        for j, weight in enumerate([gate_ref, up_ref]):
            copies[2 * i + j].wait()
            total[:, pl.ds(256 * (2 * i + j), weight.shape[1])] = contract(
                own_ref[:, :width], weight[i]
            )


def late_kernel(
    far,
    place,
    own_ref,
    half_ref,
    came_ref,
    out_maps_ref,
    total,
    down_hbm,
    sum_ref,
    maps_ref,
    down_ref,
    hidden_ref,
    sem,
):
    core = place[0]
    first = place[1] - core
    units = out_maps_ref.shape[0]
    rank = out_maps_ref.shape[1] // 2
    width = maps_ref.shape[0]
    fetch = pltpu.make_async_copy(down_hbm, down_ref, sem)
    fetch.start()

    def put(line, two, rows):
        at = 64 * line + 32 * (1 - core) + 16 * two
        maps_ref[pl.ds(pl.multiple_of(at, 16), 16), :] = rows

    def mine(line, carry):
        at = pl.ds(pl.multiple_of(64 * line + 32 * core, 32), 32)
        maps_ref[at, :] = half_ref[pl.ds(pl.multiple_of(32 * line, 32), 32), :]
        return carry

    lax.fori_loop(0, width // 64, mine, 0)
    for i in range(8):
        lay_half(far, came_ref, 0, put, i)
    low = matmul(own_ref[:, :width], maps_ref[...], False).astype(bf16)
    parts = own_ref[:, width + 1024 :].astype(f32)
    lane = lax.broadcasted_iota(jnp.int32, parts.shape, 1)
    mine_maps = out_maps_ref[...]
    their_maps = came_ref[:units, 1024:]
    for i in range(2):
        out_maps = jnp.where(core == i, mine_maps, their_maps)
        gate = total[:, 512 * i : 512 * i + units] + adapter_scale * contract(
            low[:, :rank], out_maps[:, :rank]
        )
        up = total[:, 512 * i + 256 : 512 * i + 256 + units] + adapter_scale * contract(
            low[:, rank:], out_maps[:, rank:]
        )
        at = lane - 3 * (first + i)
        named = (at >= 0) & (at < 3)
        weight = jnp.sum(jnp.where(named, parts, 0.0), axis=1, keepdims=True)
        hidden_ref[i] = (jax.nn.silu(gate) * up * weight).astype(bf16)
    fetch.wait()
    sum_ref[...] = (
        matmul(hidden_ref[0], down_ref[0], False)
        + matmul(hidden_ref[1], down_ref[1], False)
    ).astype(bf16)


def on_device(
    tokens,
    routes,
    routing_weight,
    gate_weight,
    up_weight,
    down_weight,
    adapter_input_maps,
    adapter_output_maps,
):
    chips, cores = lax.axis_size("x"), lax.axis_size("core")
    far = (lax.axis_size("y_far"), lax.axis_size("z_far"))
    few = far[0] * far[1]
    groups = chips * 4
    core = lax.axis_index("core")
    expert = lax.axis_index("x") * cores + core
    width = tokens.shape[2]
    units = gate_weight.shape[1]
    piece = width // 8
    count = groups * few

    gate, up, down = [
        lax.all_gather(w, "core", axis=0, tiled=True)
        for w in (gate_weight, up_weight, down_weight)
    ]
    place = jnp.stack([core, expert]).astype(jnp.int32)
    (blocks,) = on_core(
        block_kernel,
        (((few, 8, piece + 256), bf16),),
        (
            pltpu.SMEM(routes.shape[:0:-1], jnp.int32),
            pltpu.SMEM(routes.shape[:0:-1], f32),
            pltpu.VMEM((1, width), bf16),
            pltpu.VMEM(adapter_input_maps.shape, bf16),
            pltpu.VMEM(adapter_input_maps.shape, f32),
            pltpu.SemaphoreType.DMA((4,)),
        ),
        1,
        0,
        4,
    )(
        place,
        far_held(routes[0].T),
        far_held(routing_weight[0].T),
        far_held(tokens[0]),
        far_held(adapter_input_maps),
    )
    got = lax.all_to_all(blocks, FAR, 0, 0, tiled=True)
    rows = got[:, :, :piece].reshape(few, width)
    maps_tiles = (
        got[:, :, piece : piece + 128]
        .reshape(few // 8, 8, 8, 128)
        .transpose(0, 2, 1, 3)
        .reshape(few, 1024)
    )
    packed = jnp.concatenate([rows, maps_tiles, got[:, 0, piece + 128 :]], axis=1)
    own = spread(packed, NEAR, groups).reshape(count, -1)

    out_maps = adapter_output_maps[0].T
    other = jnp.concatenate(
        [
            own[:, width : width + 1024],
            jnp.pad(out_maps, ((0, count - units), (0, 0))),
        ],
        axis=1,
    )
    came = lax.ppermute(other, "core", [(0, 1), (1, 0)])
    own = held(own)
    total = ((count, 1024), f32)
    base, half = on_core(
        functools.partial(early_kernel, far),
        (total, ((width // 2, 128), bf16)),
        (
            pltpu.VMEM(gate.shape, bf16),
            pltpu.VMEM(up.shape, bf16),
            pltpu.SemaphoreType.DMA((4,)),
        ),
        0,
        1,
        2,
    )(own, far_held(gate), far_held(up))
    (both,) = on_core(
        functools.partial(late_kernel, far),
        (((count, width), bf16),),
        (
            pltpu.VMEM((width, 128), bf16),
            pltpu.VMEM(down.shape, bf16),
            pltpu.VMEM((2, count, units), bf16),
            pltpu.SemaphoreType.DMA,
        ),
        1,
        5,
        1,
    )(place, own, held(half), held(came), held(out_maps), held(base), far_held(down))
    near = lax.all_to_all(both, NEAR, 0, 0, tiled=True).reshape(groups, few, width)
    column = jnp.sum(near.astype(f32), axis=0).astype(bf16)
    whole = lax.all_to_all(column.reshape(few, 8, piece), FAR, 0, 0, tiled=True)
    mixed = jnp.sum(whole.astype(f32), axis=0).astype(bf16)
    return mixed.reshape(1, 1, width)


def solution(mesh):
    expert, line = mesh.devices.shape
    fine = Mesh(
        mesh.devices.reshape(expert // 2, 2, line // 16, 2, 4, 2),
        ("x", "core") + LINE,
    )
    wide = ("x", "core")
    in_specs = (
        P(LINE, wide, None),
        P(LINE, None, None),
        P(LINE, None, None),
        P(wide, LINE, None),
        P(wide, LINE, None),
        P(wide, LINE, None),
        P(LINE, None),
        P(wide, None, LINE),
    )
    return jax.shard_map(
        on_device, mesh=fine, in_specs=in_specs, out_specs=P(LINE, wide, None), check_vma=False
    )
```

```python
import functools

import jax
import jax.numpy as jnp
from jax import lax
from jax.experimental import pallas as pl
from jax.experimental.pallas import tpu as pltpu
from jax.sharding import Mesh, PartitionSpec as P

adapter_scale = 0.5
LINE = ("y_far", "y_near", "z_far", "z_near")
FAR = ("y_far", "z_far")
NEAR = ("x", "y_near", "z_near")
VMEM = pl.BlockSpec(memory_space=pltpu.VMEM)
HBM = pl.BlockSpec(memory_space=pltpu.HBM)
SMEM = pl.BlockSpec(memory_space=pltpu.SMEM)
bf16, f32 = jnp.bfloat16, jnp.float32


def held(array):
    return pltpu.with_memory_space_constraint(array, pltpu.VMEM)


def far_held(array):
    return pltpu.with_memory_space_constraint(array, pltpu.HBM)


def on_core(kernel, outs, scratch=(), placed=0, arrays=0, far=0):
    return pl.pallas_call(
        kernel,
        in_specs=[SMEM] * placed + [VMEM] * arrays + [HBM] * far,
        out_specs=tuple(VMEM for _ in outs),
        out_shape=tuple(pltpu.VMEM(shape, kind) for shape, kind in outs),
        scratch_shapes=scratch,
        compiler_params=pltpu.CompilerParams(vmem_limit_bytes=16 << 20),
    )


def matmul(left, right, transposed):
    side = ((1,), (1 if transposed else 0,))
    return lax.dot_general(left, right, (side, ((), ())), preferred_element_type=f32)


def contract(left, right):
    return matmul(left, right, True)


def spread(block, axes, count):
    return lax.all_to_all(
        jnp.broadcast_to(block[None], (count,) + block.shape), axes, 0, 0, tiled=True
    )


def block_kernel(
    place,
    routes_hbm,
    weights_hbm,
    token_hbm,
    maps_hbm,
    gate_hbm,
    up_hbm,
    down_hbm,
    block_ref,
    held_ref,
    routes,
    weights,
    token_ref,
    maps_ref,
    rows,
    sems,
):
    copies = [
        pltpu.make_async_copy(source, target, sems.at[i])
        for i, (source, target) in enumerate(
            [
                (routes_hbm, routes),
                (weights_hbm, weights),
                (token_hbm, token_ref),
                (maps_hbm, maps_ref),
            ]
        )
    ]
    units = gate_hbm.shape[0]
    fetches = [
        pltpu.make_async_copy(
            source, held_ref.at[pl.ds(i * units, units)], sems.at[4 + i]
        )
        for i, source in enumerate([gate_hbm, up_hbm, down_hbm])
    ]
    for copy in copies + fetches:
        copy.start()
    for copy in copies:
        copy.wait()
    core, expert = place[0], place[1]
    piece = token_ref.shape[1] // 8
    token = token_ref[...].astype(f32)
    token = jnp.concatenate(
        [token[:, s * piece : (s + 1) * piece] for s in range(8)], axis=0
    )
    rows[...] = maps_ref[...].astype(f32)
    start = 32 * core + 8 * (expert // 2)
    share = rows[pl.ds(pl.multiple_of(start, 8), 8), :]
    lane = lax.broadcasted_iota(jnp.int32, (8, 128), 1)
    first = lax.broadcasted_iota(jnp.int32, (8, 128), 0) == 0
    extra = jnp.zeros((8, 128), f32)
    for use in range(routes.shape[0]):
        weight = jnp.full((8, 128), weights[use, expert], f32)
        high = weight.astype(bf16).astype(f32)
        rest = weight - high
        middle = rest.astype(bf16).astype(f32)
        at = jnp.where(first, lane - 3 * routes[use, expert], -1)
        extra = jnp.where(at == 0, high, extra)
        extra = jnp.where(at == 1, middle, extra)
        extra = jnp.where(at == 2, rest - middle, extra)
    block = jnp.concatenate([token, share, extra], axis=1).astype(bf16)
    block_ref[...] = jnp.broadcast_to(block[None], block_ref.shape)
    for fetch in fetches:
        fetch.wait()


def lay_half(far, rows_ref, start, put, i):
    far_y, far_z = far
    count = far_y * far_z
    pairs = count // 16
    near, two = i // 2, i % 2
    near_y, near_z = near // 2, near % 2
    for pair in range(pairs):

        def rows_of(chip):
            return pl.ds((chip * 4 + near) * count + pair * 16, 16)

        for b in range(8):
            lanes = slice(start + b * 128, start + (b + 1) * 128)
            low = rows_ref[rows_of(2 * two), lanes].astype(f32)
            high = rows_ref[rows_of(2 * two + 1), lanes].astype(f32)
            for half in range(2):
                place = 8 * (2 * pair + half) + b
                y, z = 2 * (place // far_z) + near_y, 2 * (place % far_z) + near_z
                part = slice(8 * half, 8 * half + 8)
                put(
                    y * 2 * far_z + z,
                    two,
                    jnp.concatenate([low[part], high[part]], axis=0).astype(bf16),
                )


def early_kernel(far, own_ref, mine_ref, other_ref, total, half_ref):
    both = mine_ref.shape[0] // 3 * 2
    width = mine_ref.shape[1]

    def put(line, two, rows):
        half_ref[pl.ds(32 * line + 16 * two, 16), :] = rows

    for i in range(8):
        lay_half(far, own_ref, width, put, i)
    for i, weights in enumerate([mine_ref, other_ref]):
        total[:, 512 * i : 512 * i + both] = contract(
            own_ref[:, :width], weights[:both, :]
        )


def late_kernel(
    far,
    place,
    own_ref,
    half_ref,
    came_ref,
    out_maps_ref,
    total,
    mine_ref,
    other_ref,
    sum_ref,
    maps_ref,
):
    core = place[0]
    units = out_maps_ref.shape[0]
    rank = out_maps_ref.shape[1] // 2
    width = maps_ref.shape[0]

    def put(line, two, rows):
        at = 64 * line + 32 * (1 - core) + 16 * two
        maps_ref[pl.ds(pl.multiple_of(at, 16), 16), :] = rows

    def mine(line, carry):
        at = pl.ds(pl.multiple_of(64 * line + 32 * core, 32), 32)
        maps_ref[at, :] = half_ref[pl.ds(pl.multiple_of(32 * line, 32), 32), :]
        return carry

    lax.fori_loop(0, width // 64, mine, 0)
    for i in range(8):
        lay_half(far, came_ref, 0, put, i)
    low = matmul(own_ref[:, :width], maps_ref[...], False).astype(bf16)
    parts = own_ref[:, width + 1024 :].astype(f32)
    lane = lax.broadcasted_iota(jnp.int32, parts.shape, 1)
    result = None
    for i, (expert, out_maps, down) in enumerate(
        [
            (place[1], out_maps_ref[...], mine_ref),
            (place[1] + 1 - 2 * core, came_ref[:units, 1024:], other_ref),
        ]
    ):
        at = 512 * i
        gate = total[:, at : at + units] + adapter_scale * contract(
            low[:, :rank], out_maps[:, :rank]
        )
        up = total[:, at + units : at + 2 * units] + adapter_scale * contract(
            low[:, rank:], out_maps[:, rank:]
        )
        named = (lane >= 3 * expert) & (lane < 3 * expert + 3)
        weight = jnp.sum(jnp.where(named, parts, 0.0), axis=1, keepdims=True)
        hidden = (jax.nn.silu(gate) * up * weight).astype(bf16)
        part = matmul(hidden, down[2 * units :, :], False)
        result = part if result is None else result + part
    sum_ref[...] = result.astype(bf16)


def on_device(
    tokens,
    routes,
    routing_weight,
    gate_weight,
    up_weight,
    down_weight,
    adapter_input_maps,
    adapter_output_maps,
):
    chips, cores = lax.axis_size("x"), lax.axis_size("core")
    far = (lax.axis_size("y_far"), lax.axis_size("z_far"))
    few = far[0] * far[1]
    groups = chips * 4
    core = lax.axis_index("core")
    expert = lax.axis_index("x") * cores + core
    width = tokens.shape[2]
    units = gate_weight.shape[1]
    piece = width // 8
    count = groups * few

    place = jnp.stack([core, expert]).astype(jnp.int32)
    blocks, weights = on_core(
        block_kernel,
        (((few, 8, piece + 256), bf16), ((3 * units, width), bf16)),
        (
            pltpu.SMEM(routes.shape[:0:-1], jnp.int32),
            pltpu.SMEM(routes.shape[:0:-1], f32),
            pltpu.VMEM((1, width), bf16),
            pltpu.VMEM(adapter_input_maps.shape, bf16),
            pltpu.VMEM(adapter_input_maps.shape, f32),
            pltpu.SemaphoreType.DMA((7,)),
        ),
        1,
        0,
        7,
    )(
        place,
        far_held(routes[0].T),
        far_held(routing_weight[0].T),
        far_held(tokens[0]),
        far_held(adapter_input_maps),
        far_held(gate_weight[0]),
        far_held(up_weight[0]),
        far_held(down_weight[0]),
    )
    swap = [(0, 1), (1, 0)]
    other_weights = lax.ppermute(weights, "core", swap)
    got = lax.all_to_all(blocks, FAR, 0, 0, tiled=True)
    rows = got[:, :, :piece].reshape(few, width)
    maps_tiles = (
        got[:, :, piece : piece + 128]
        .reshape(few // 8, 8, 8, 128)
        .transpose(0, 2, 1, 3)
        .reshape(few, 1024)
    )
    packed = jnp.concatenate([rows, maps_tiles, got[:, 0, piece + 128 :]], axis=1)
    own = spread(packed, NEAR, groups).reshape(count, -1)

    out_maps = adapter_output_maps[0].T
    other = jnp.concatenate(
        [
            own[:, width : width + 1024],
            jnp.pad(out_maps, ((0, count - units), (0, 0))),
        ],
        axis=1,
    )
    came = lax.ppermute(other, "core", swap)
    own, weights, other_weights = held(own), held(weights), held(other_weights)
    base, half = on_core(
        functools.partial(early_kernel, far),
        (((count, 1024), f32), ((width // 2, 128), bf16)),
        (),
        0,
        3,
    )(own, weights, other_weights)
    (both,) = on_core(
        functools.partial(late_kernel, far),
        (((count, width), bf16),),
        (pltpu.VMEM((width, 128), bf16),),
        1,
        7,
    )(
        place,
        own,
        held(half),
        held(came),
        held(out_maps),
        held(base),
        weights,
        other_weights,
    )
    near = lax.all_to_all(both, NEAR, 0, 0, tiled=True).reshape(groups, few, width)
    column = jnp.sum(near.astype(f32), axis=0).astype(bf16)
    whole = lax.all_to_all(column.reshape(few, 8, piece), FAR, 0, 0, tiled=True)
    mixed = jnp.sum(whole.astype(f32), axis=0).astype(bf16)
    return mixed.reshape(1, 1, width)


def solution(mesh):
    expert, line = mesh.devices.shape
    fine = Mesh(
        mesh.devices.reshape(expert // 2, 2, line // 16, 2, 4, 2),
        ("x", "core") + LINE,
    )
    wide = ("x", "core")
    in_specs = (
        P(LINE, wide, None),
        P(LINE, None, None),
        P(LINE, None, None),
        P(wide, LINE, None),
        P(wide, LINE, None),
        P(wide, LINE, None),
        P(LINE, None),
        P(wide, None, LINE),
    )
    return jax.shard_map(
        on_device, mesh=fine, in_specs=in_specs, out_specs=P(LINE, wide, None), check_vma=False
    )
```

```python
import functools

import jax
import jax.numpy as jnp
from jax import lax
from jax.experimental import pallas as pl
from jax.experimental.pallas import tpu as pltpu
from jax.sharding import Mesh, PartitionSpec as P

adapter_scale = 0.5
LINE = ("y_far", "y_near", "z_far", "z_near")
FAR = ("y_far", "z_far")
NEAR = ("x", "y_near", "z_near")
VMEM = pl.BlockSpec(memory_space=pltpu.VMEM)
HBM = pl.BlockSpec(memory_space=pltpu.HBM)
ANY = pl.BlockSpec(memory_space=pl.ANY)
SMEM = pl.BlockSpec(memory_space=pltpu.SMEM)
bf16, f32 = jnp.bfloat16, jnp.float32


def held(array):
    return pltpu.with_memory_space_constraint(array, pltpu.VMEM)


def far_held(array):
    return pltpu.with_memory_space_constraint(array, pltpu.HBM)


def on_core(kernel, outs, scratch=(), placed=0, arrays=0, far=0, free=0):
    return pl.pallas_call(
        kernel,
        in_specs=[SMEM] * placed + [VMEM] * arrays + [HBM] * far + [ANY] * free,
        out_specs=tuple(VMEM for _ in outs),
        out_shape=tuple(pltpu.VMEM(shape, kind) for shape, kind in outs),
        scratch_shapes=scratch,
        compiler_params=pltpu.CompilerParams(vmem_limit_bytes=20 << 20),
    )


def matmul(left, right, transposed):
    side = ((1,), (1 if transposed else 0,))
    return lax.dot_general(left, right, (side, ((), ())), preferred_element_type=f32)


def contract(left, right):
    return matmul(left, right, True)


def spread(block, axes, count):
    return lax.all_to_all(
        jnp.broadcast_to(block[None], (count,) + block.shape), axes, 0, 0, tiled=True
    )


def block_kernel(
    place,
    routes_hbm,
    weights_hbm,
    token_hbm,
    maps_hbm,
    block_ref,
    routes,
    weights,
    token_ref,
    maps_ref,
    rows,
    sems,
):
    copies = [
        pltpu.make_async_copy(source, target, sems.at[i])
        for i, (source, target) in enumerate(
            [
                (routes_hbm, routes),
                (weights_hbm, weights),
                (token_hbm, token_ref),
                (maps_hbm, maps_ref),
            ]
        )
    ]
    for copy in copies:
        copy.start()
    for copy in copies:
        copy.wait()
    core, expert = place[0], place[1]
    piece = token_ref.shape[1] // 8
    token = token_ref[...].astype(f32)
    token = jnp.concatenate(
        [token[:, s * piece : (s + 1) * piece] for s in range(8)], axis=0
    )
    rows[...] = maps_ref[...].astype(f32)
    start = 32 * core + 8 * (expert // 2)
    share = rows[pl.ds(pl.multiple_of(start, 8), 8), :]
    lane = lax.broadcasted_iota(jnp.int32, (8, 128), 1)
    first = lax.broadcasted_iota(jnp.int32, (8, 128), 0) == 0
    extra = jnp.zeros((8, 128), f32)
    for use in range(routes.shape[0]):
        weight = jnp.full((8, 128), weights[use, expert], f32)
        high = weight.astype(bf16).astype(f32)
        rest = weight - high
        middle = rest.astype(bf16).astype(f32)
        at = jnp.where(first, lane - 3 * routes[use, expert], -1)
        extra = jnp.where(at == 0, high, extra)
        extra = jnp.where(at == 1, middle, extra)
        extra = jnp.where(at == 2, rest - middle, extra)
    block = jnp.concatenate([token, share, extra], axis=1).astype(bf16)
    block_ref[...] = jnp.broadcast_to(block[None], block_ref.shape)


def lay_half(far, rows_ref, start, put, i):
    far_y, far_z = far
    count = far_y * far_z
    pairs = count // 16
    near, two = i // 2, i % 2
    near_y, near_z = near // 2, near % 2
    for pair in range(pairs):

        def rows_of(chip):
            return pl.ds((chip * 4 + near) * count + pair * 16, 16)

        for b in range(8):
            lanes = slice(start + b * 128, start + (b + 1) * 128)
            low = rows_ref[rows_of(2 * two), lanes].astype(f32)
            high = rows_ref[rows_of(2 * two + 1), lanes].astype(f32)
            for half in range(2):
                place = 8 * (2 * pair + half) + b
                y, z = 2 * (place // far_z) + near_y, 2 * (place % far_z) + near_z
                part = slice(8 * half, 8 * half + 8)
                put(
                    y * 2 * far_z + z,
                    two,
                    jnp.concatenate([low[part], high[part]], axis=0).astype(bf16),
                )


def early_kernel(
    far, own_ref, gate_hbm, up_hbm, gate2_hbm, up2_hbm, total, half_ref, held_ref, sems
):
    units, width = gate_hbm.shape
    copies = [
        pltpu.make_async_copy(
            source, held_ref.at[i // 2, pl.ds(i % 2 * units, units)], sems.at[i]
        )
        for i, source in enumerate([gate_hbm, up_hbm, gate2_hbm, up2_hbm])
    ]
    for copy in copies:
        copy.start()

    def put(line, two, rows):
        half_ref[pl.ds(32 * line + 16 * two, 16), :] = rows

    for i in range(8):
        lay_half(far, own_ref, width, put, i)
    for i in range(2):
        copies[2 * i].wait()
        copies[2 * i + 1].wait()
        total[:, 512 * i : 512 * i + 2 * units] = contract(
            own_ref[:, :width], held_ref[i]
        )


def late_kernel(
    far,
    place,
    own_ref,
    half_ref,
    came_ref,
    out_maps_ref,
    total,
    down_hbm,
    down2_hbm,
    sum_ref,
    maps_ref,
    down_ref,
    sems,
):
    core = place[0]
    units = out_maps_ref.shape[0]
    rank = out_maps_ref.shape[1] // 2
    width = maps_ref.shape[0]
    copies = [
        pltpu.make_async_copy(source, down_ref.at[i], sems.at[i])
        for i, source in enumerate([down_hbm, down2_hbm])
    ]
    for copy in copies:
        copy.start()

    def put(line, two, rows):
        at = 64 * line + 32 * (1 - core) + 16 * two
        maps_ref[pl.ds(pl.multiple_of(at, 16), 16), :] = rows

    def mine(line, carry):
        at = pl.ds(pl.multiple_of(64 * line + 32 * core, 32), 32)
        maps_ref[at, :] = half_ref[pl.ds(pl.multiple_of(32 * line, 32), 32), :]
        return carry

    lax.fori_loop(0, width // 64, mine, 0)
    for i in range(8):
        lay_half(far, came_ref, 0, put, i)
    low = matmul(own_ref[:, :width], maps_ref[...], False).astype(bf16)
    parts = own_ref[:, width + 1024 :].astype(f32)
    lane = lax.broadcasted_iota(jnp.int32, parts.shape, 1)
    result = None
    for i, (expert, out_maps) in enumerate(
        [
            (place[1], out_maps_ref[...]),
            (place[1] + 1 - 2 * core, came_ref[:units, 1024:]),
        ]
    ):
        at = 512 * i
        gate = total[:, at : at + units] + adapter_scale * contract(
            low[:, :rank], out_maps[:, :rank]
        )
        up = total[:, at + units : at + 2 * units] + adapter_scale * contract(
            low[:, rank:], out_maps[:, rank:]
        )
        named = (lane >= 3 * expert) & (lane < 3 * expert + 3)
        weight = jnp.sum(jnp.where(named, parts, 0.0), axis=1, keepdims=True)
        hidden = (jax.nn.silu(gate) * up * weight).astype(bf16)
        copies[i].wait()
        part = matmul(hidden, down_ref[i], False)
        result = part if result is None else result + part
    sum_ref[...] = result.astype(bf16)


def on_device(
    tokens,
    routes,
    routing_weight,
    gate_weight,
    up_weight,
    down_weight,
    adapter_input_maps,
    adapter_output_maps,
):
    chips, cores = lax.axis_size("x"), lax.axis_size("core")
    far = (lax.axis_size("y_far"), lax.axis_size("z_far"))
    few = far[0] * far[1]
    groups = chips * 4
    core = lax.axis_index("core")
    expert = lax.axis_index("x") * cores + core
    width = tokens.shape[2]
    units = gate_weight.shape[1]
    piece = width // 8
    count = groups * few

    place = jnp.stack([core, expert]).astype(jnp.int32)
    (blocks,) = on_core(
        block_kernel,
        (((few, 8, piece + 256), bf16),),
        (
            pltpu.SMEM(routes.shape[:0:-1], jnp.int32),
            pltpu.SMEM(routes.shape[:0:-1], f32),
            pltpu.VMEM((1, width), bf16),
            pltpu.VMEM(adapter_input_maps.shape, bf16),
            pltpu.VMEM(adapter_input_maps.shape, f32),
            pltpu.SemaphoreType.DMA((4,)),
        ),
        1,
        0,
        4,
    )(
        place,
        far_held(routes[0].T),
        far_held(routing_weight[0].T),
        far_held(tokens[0]),
        far_held(adapter_input_maps),
    )
    got = lax.all_to_all(blocks, FAR, 0, 0, tiled=True)
    swap = [(0, 1), (1, 0)]
    mine = [w[0] for w in (gate_weight, up_weight, down_weight)]
    got, *sent = lax.optimization_barrier((got, *mine))
    others = [lax.ppermute(w, "core", swap) for w in sent]
    rows = got[:, :, :piece].reshape(few, width)
    maps_tiles = (
        got[:, :, piece : piece + 128]
        .reshape(few // 8, 8, 8, 128)
        .transpose(0, 2, 1, 3)
        .reshape(few, 1024)
    )
    packed = jnp.concatenate([rows, maps_tiles, got[:, 0, piece + 128 :]], axis=1)
    own = spread(packed, NEAR, groups).reshape(count, -1)

    out_maps = adapter_output_maps[0].T
    other = jnp.concatenate(
        [
            own[:, width : width + 1024],
            jnp.pad(out_maps, ((0, count - units), (0, 0))),
        ],
        axis=1,
    )
    came = lax.ppermute(other, "core", swap)
    own = held(own)
    gate, up, down = [far_held(w) for w in mine]
    gate2, up2, down2 = others
    base, half = on_core(
        functools.partial(early_kernel, far),
        (((count, 1024), f32), ((width // 2, 128), bf16)),
        (pltpu.VMEM((2, 2 * units, width), bf16), pltpu.SemaphoreType.DMA((4,))),
        0,
        1,
        2,
        2,
    )(own, gate, up, gate2, up2)
    (both,) = on_core(
        functools.partial(late_kernel, far),
        (((count, width), bf16),),
        (
            pltpu.VMEM((width, 128), bf16),
            pltpu.VMEM((2, units, width), bf16),
            pltpu.SemaphoreType.DMA((2,)),
        ),
        1,
        5,
        1,
        1,
    )(place, own, held(half), held(came), held(out_maps), held(base), down, down2)
    near = lax.all_to_all(both, NEAR, 0, 0, tiled=True).reshape(groups, few, width)
    column = jnp.sum(near.astype(f32), axis=0).astype(bf16)
    whole = lax.all_to_all(column.reshape(few, 8, piece), FAR, 0, 0, tiled=True)
    mixed = jnp.sum(whole.astype(f32), axis=0).astype(bf16)
    return mixed.reshape(1, 1, width)


def solution(mesh):
    expert, line = mesh.devices.shape
    fine = Mesh(
        mesh.devices.reshape(expert // 2, 2, line // 16, 2, 4, 2),
        ("x", "core") + LINE,
    )
    wide = ("x", "core")
    in_specs = (
        P(LINE, wide, None),
        P(LINE, None, None),
        P(LINE, None, None),
        P(wide, LINE, None),
        P(wide, LINE, None),
        P(wide, LINE, None),
        P(LINE, None),
        P(wide, None, LINE),
    )
    return jax.shard_map(
        on_device, mesh=fine, in_specs=in_specs, out_specs=P(LINE, wide, None), check_vma=False
    )
```

```python
import functools

import jax
import jax.numpy as jnp
from jax import lax
from jax.experimental import pallas as pl
from jax.experimental.pallas import tpu as pltpu
from jax.sharding import Mesh, PartitionSpec as P

adapter_scale = 0.5
LINE = ("y_far", "y_near", "z_far", "z_near")
FAR = ("y_far", "z_far")
NEAR = ("x", "y_near", "z_near")
VMEM = pl.BlockSpec(memory_space=pltpu.VMEM)
HBM = pl.BlockSpec(memory_space=pltpu.HBM)
SMEM = pl.BlockSpec(memory_space=pltpu.SMEM)
bf16, f32 = jnp.bfloat16, jnp.float32


def held(array):
    return pltpu.with_memory_space_constraint(array, pltpu.VMEM)


def far_held(array):
    return pltpu.with_memory_space_constraint(array, pltpu.HBM)


def on_core(kernel, outs, scratch=(), placed=0, arrays=0, far=0):
    return pl.pallas_call(
        kernel,
        in_specs=[SMEM] * placed + [VMEM] * arrays + [HBM] * far,
        out_specs=tuple(VMEM for _ in outs),
        out_shape=tuple(pltpu.VMEM(shape, kind) for shape, kind in outs),
        scratch_shapes=scratch,
        compiler_params=pltpu.CompilerParams(vmem_limit_bytes=16 << 20),
    )


def matmul(left, right, transposed):
    side = ((1,), (1 if transposed else 0,))
    return lax.dot_general(left, right, (side, ((), ())), preferred_element_type=f32)


def contract(left, right):
    return matmul(left, right, True)


def spread(block, axes, count):
    return lax.all_to_all(
        jnp.broadcast_to(block[None], (count,) + block.shape), axes, 0, 0, tiled=True
    )


def block_kernel(
    place,
    routes_hbm,
    weights_hbm,
    token_hbm,
    maps_hbm,
    gate_hbm,
    up_hbm,
    down_hbm,
    block_ref,
    held_ref,
    routes,
    weights,
    token_ref,
    maps_ref,
    rows,
    sems,
):
    copies = [
        pltpu.make_async_copy(source, target, sems.at[i])
        for i, (source, target) in enumerate(
            [
                (routes_hbm, routes),
                (weights_hbm, weights),
                (token_hbm, token_ref),
                (maps_hbm, maps_ref),
            ]
        )
    ]
    units = gate_hbm.shape[0]
    fetches = [
        pltpu.make_async_copy(
            source, held_ref.at[pl.ds(i * units, units)], sems.at[4 + i]
        )
        for i, source in enumerate([gate_hbm, up_hbm, down_hbm])
    ]
    for copy in copies + fetches:
        copy.start()
    for copy in copies:
        copy.wait()
    core, expert = place[0], place[1]
    piece = token_ref.shape[1] // 8
    token = token_ref[...].astype(f32)
    token = jnp.concatenate(
        [token[:, s * piece : (s + 1) * piece] for s in range(8)], axis=0
    )
    rows[...] = maps_ref[...].astype(f32)
    start = 32 * core + 8 * (expert // 2)
    share = rows[pl.ds(pl.multiple_of(start, 8), 8), :]
    lane = lax.broadcasted_iota(jnp.int32, (8, 128), 1)
    first = lax.broadcasted_iota(jnp.int32, (8, 128), 0) == 0
    extra = jnp.zeros((8, 128), f32)
    for use in range(routes.shape[0]):
        weight = jnp.full((8, 128), weights[use, expert], f32)
        high = weight.astype(bf16).astype(f32)
        rest = weight - high
        middle = rest.astype(bf16).astype(f32)
        at = jnp.where(first, lane - 3 * routes[use, expert], -1)
        extra = jnp.where(at == 0, high, extra)
        extra = jnp.where(at == 1, middle, extra)
        extra = jnp.where(at == 2, rest - middle, extra)
    block = jnp.concatenate([token, share, extra], axis=1).astype(bf16)
    block_ref[...] = jnp.broadcast_to(block[None], block_ref.shape)
    for fetch in fetches:
        fetch.wait()


def lay_half(far, rows_ref, start, put, i):
    far_y, far_z = far
    count = far_y * far_z
    pairs = count // 16
    near, two = i // 2, i % 2
    near_y, near_z = near // 2, near % 2
    for pair in range(pairs):

        def rows_of(chip):
            return pl.ds((chip * 4 + near) * count + pair * 16, 16)

        for b in range(8):
            lanes = slice(start + b * 128, start + (b + 1) * 128)
            low = rows_ref[rows_of(2 * two), lanes].astype(f32)
            high = rows_ref[rows_of(2 * two + 1), lanes].astype(f32)
            for half in range(2):
                place = 8 * (2 * pair + half) + b
                y, z = 2 * (place // far_z) + near_y, 2 * (place % far_z) + near_z
                part = slice(8 * half, 8 * half + 8)
                put(
                    y * 2 * far_z + z,
                    two,
                    jnp.concatenate([low[part], high[part]], axis=0).astype(bf16),
                )


def early_kernel(far, own_ref, mine_ref, other_ref, total, half_ref):
    both = mine_ref.shape[0] // 3 * 2
    width = mine_ref.shape[1]

    def put(line, two, rows):
        half_ref[pl.ds(32 * line + 16 * two, 16), :] = rows

    for i in range(8):
        lay_half(far, own_ref, width, put, i)
    for i, weights in enumerate([mine_ref, other_ref]):
        total[:, 512 * i : 512 * i + both] = contract(
            own_ref[:, :width], weights[:both, :]
        )


def late_kernel(
    far,
    place,
    own_ref,
    half_ref,
    came_ref,
    out_maps_ref,
    total,
    mine_ref,
    other_ref,
    sum_ref,
    maps_ref,
):
    core = place[0]
    units = out_maps_ref.shape[0]
    rank = out_maps_ref.shape[1] // 2
    width = maps_ref.shape[0]

    def put(line, two, rows):
        at = 64 * line + 32 * (1 - core) + 16 * two
        maps_ref[pl.ds(pl.multiple_of(at, 16), 16), :] = rows

    def mine(line, carry):
        at = pl.ds(pl.multiple_of(64 * line + 32 * core, 32), 32)
        maps_ref[at, :] = half_ref[pl.ds(pl.multiple_of(32 * line, 32), 32), :]
        return carry

    lax.fori_loop(0, width // 64, mine, 0)
    for i in range(8):
        lay_half(far, came_ref, 0, put, i)
    low = matmul(own_ref[:, :width], maps_ref[...], False).astype(bf16)
    parts = own_ref[:, width + 1024 :].astype(f32)
    lane = lax.broadcasted_iota(jnp.int32, parts.shape, 1)
    result = None
    for i, (expert, out_maps, down) in enumerate(
        [
            (place[1], out_maps_ref[...], mine_ref),
            (place[1] + 1 - 2 * core, came_ref[:units, 1024:], other_ref),
        ]
    ):
        at = 512 * i
        gate = total[:, at : at + units] + adapter_scale * contract(
            low[:, :rank], out_maps[:, :rank]
        )
        up = total[:, at + units : at + 2 * units] + adapter_scale * contract(
            low[:, rank:], out_maps[:, rank:]
        )
        named = (lane >= 3 * expert) & (lane < 3 * expert + 3)
        weight = jnp.sum(jnp.where(named, parts, 0.0), axis=1, keepdims=True)
        hidden = (jax.nn.silu(gate) * up * weight).astype(bf16)
        part = matmul(hidden, down[2 * units :, :], False)
        result = part if result is None else result + part
    sum_ref[...] = result.astype(bf16)


def on_device(
    tokens,
    routes,
    routing_weight,
    gate_weight,
    up_weight,
    down_weight,
    adapter_input_maps,
    adapter_output_maps,
):
    chips, cores = lax.axis_size("x"), lax.axis_size("core")
    far = (lax.axis_size("y_far"), lax.axis_size("z_far"))
    few = far[0] * far[1]
    groups = chips * 4
    core = lax.axis_index("core")
    expert = lax.axis_index("x") * cores + core
    width = tokens.shape[2]
    units = gate_weight.shape[1]
    piece = width // 8
    count = groups * few

    place = jnp.stack([core, expert]).astype(jnp.int32)
    blocks, weights = on_core(
        block_kernel,
        (((few, 8, piece + 256), bf16), ((3 * units, width), bf16)),
        (
            pltpu.SMEM(routes.shape[:0:-1], jnp.int32),
            pltpu.SMEM(routes.shape[:0:-1], f32),
            pltpu.VMEM((1, width), bf16),
            pltpu.VMEM(adapter_input_maps.shape, bf16),
            pltpu.VMEM(adapter_input_maps.shape, f32),
            pltpu.SemaphoreType.DMA((7,)),
        ),
        1,
        0,
        7,
    )(
        place,
        far_held(routes[0].T),
        far_held(routing_weight[0].T),
        far_held(tokens[0]),
        far_held(adapter_input_maps),
        far_held(gate_weight[0]),
        far_held(up_weight[0]),
        far_held(down_weight[0]),
    )
    swap = [(0, 1), (1, 0)]
    other_weights = lax.ppermute(weights, "core", swap)
    got = lax.all_to_all(blocks, FAR, 0, 0, tiled=True)
    got, other_weights = lax.optimization_barrier((got, other_weights))
    rows = got[:, :, :piece].reshape(few, width)
    maps_tiles = (
        got[:, :, piece : piece + 128]
        .reshape(few // 8, 8, 8, 128)
        .transpose(0, 2, 1, 3)
        .reshape(few, 1024)
    )
    packed = jnp.concatenate([rows, maps_tiles, got[:, 0, piece + 128 :]], axis=1)
    own = spread(packed, NEAR, groups).reshape(count, -1)

    out_maps = adapter_output_maps[0].T
    other = jnp.concatenate(
        [
            own[:, width : width + 1024],
            jnp.pad(out_maps, ((0, count - units), (0, 0))),
        ],
        axis=1,
    )
    came = lax.ppermute(other, "core", swap)
    own, weights, other_weights = held(own), held(weights), held(other_weights)
    base, half = on_core(
        functools.partial(early_kernel, far),
        (((count, 1024), f32), ((width // 2, 128), bf16)),
        (),
        0,
        3,
    )(own, weights, other_weights)
    (both,) = on_core(
        functools.partial(late_kernel, far),
        (((count, width), bf16),),
        (pltpu.VMEM((width, 128), bf16),),
        1,
        7,
    )(
        place,
        own,
        held(half),
        held(came),
        held(out_maps),
        held(base),
        weights,
        other_weights,
    )
    near = lax.all_to_all(both, NEAR, 0, 0, tiled=True).reshape(groups, few, width)
    column = jnp.sum(near.astype(f32), axis=0).astype(bf16)
    whole = lax.all_to_all(column.reshape(few, 8, piece), FAR, 0, 0, tiled=True)
    mixed = jnp.sum(whole.astype(f32), axis=0).astype(bf16)
    return mixed.reshape(1, 1, width)


def solution(mesh):
    expert, line = mesh.devices.shape
    fine = Mesh(
        mesh.devices.reshape(expert // 2, 2, line // 16, 2, 4, 2),
        ("x", "core") + LINE,
    )
    wide = ("x", "core")
    in_specs = (
        P(LINE, wide, None),
        P(LINE, None, None),
        P(LINE, None, None),
        P(wide, LINE, None),
        P(wide, LINE, None),
        P(wide, LINE, None),
        P(LINE, None),
        P(wide, None, LINE),
    )
    return jax.shard_map(
        on_device, mesh=fine, in_specs=in_specs, out_specs=P(LINE, wide, None), check_vma=False
    )
```

```python
import functools

import jax
import jax.numpy as jnp
from jax import lax
from jax.experimental import pallas as pl
from jax.experimental.pallas import tpu as pltpu
from jax.sharding import Mesh, PartitionSpec as P

adapter_scale = 0.5
LINE = ("y_far", "y_near", "z_far", "z_near")
FAR = ("y_far", "z_far")
NEAR = ("x", "y_near", "z_near")
VMEM = pl.BlockSpec(memory_space=pltpu.VMEM)
HBM = pl.BlockSpec(memory_space=pltpu.HBM)
SMEM = pl.BlockSpec(memory_space=pltpu.SMEM)
bf16, f32 = jnp.bfloat16, jnp.float32


def held(array):
    return pltpu.with_memory_space_constraint(array, pltpu.VMEM)


def far_held(array):
    return pltpu.with_memory_space_constraint(array, pltpu.HBM)


def on_core(kernel, outs, scratch=(), placed=0, arrays=0, far=0):
    return pl.pallas_call(
        kernel,
        in_specs=[SMEM] * placed + [VMEM] * arrays + [HBM] * far,
        out_specs=tuple(VMEM for _ in outs),
        out_shape=tuple(pltpu.VMEM(shape, kind) for shape, kind in outs),
        scratch_shapes=scratch,
        compiler_params=pltpu.CompilerParams(vmem_limit_bytes=16 << 20),
    )


def matmul(left, right, transposed):
    side = ((1,), (1 if transposed else 0,))
    return lax.dot_general(left, right, (side, ((), ())), preferred_element_type=f32)


def contract(left, right):
    return matmul(left, right, True)


def spread(block, axes, count):
    return lax.all_to_all(
        jnp.broadcast_to(block[None], (count,) + block.shape), axes, 0, 0, tiled=True
    )


def block_kernel(
    place,
    routes_hbm,
    weights_hbm,
    token_hbm,
    maps_hbm,
    gate_hbm,
    up_hbm,
    down_hbm,
    block_ref,
    held_ref,
    routes,
    weights,
    token_ref,
    maps_ref,
    rows,
    sems,
):
    copies = [
        pltpu.make_async_copy(source, target, sems.at[i])
        for i, (source, target) in enumerate(
            [
                (routes_hbm, routes),
                (weights_hbm, weights),
                (token_hbm, token_ref),
                (maps_hbm, maps_ref),
            ]
        )
    ]
    units = gate_hbm.shape[0]
    fetches = [
        pltpu.make_async_copy(
            source, held_ref.at[pl.ds(i * units, units)], sems.at[4 + i]
        )
        for i, source in enumerate([gate_hbm, up_hbm, down_hbm])
    ]
    for copy in copies + fetches:
        copy.start()
    for copy in copies:
        copy.wait()
    core, expert = place[0], place[1]
    piece = token_ref.shape[1] // 8
    token = token_ref[...].astype(f32)
    token = jnp.concatenate(
        [token[:, s * piece : (s + 1) * piece] for s in range(8)], axis=0
    )
    rows[...] = maps_ref[...].astype(f32)
    start = 32 * core + 8 * (expert // 2)
    share = rows[pl.ds(pl.multiple_of(start, 8), 8), :]
    lane = lax.broadcasted_iota(jnp.int32, (8, 128), 1)
    first = lax.broadcasted_iota(jnp.int32, (8, 128), 0) == 0
    extra = jnp.zeros((8, 128), f32)
    for use in range(routes.shape[0]):
        weight = jnp.full((8, 128), weights[use, expert], f32)
        high = weight.astype(bf16).astype(f32)
        rest = weight - high
        middle = rest.astype(bf16).astype(f32)
        at = jnp.where(first, lane - 3 * routes[use, expert], -1)
        extra = jnp.where(at == 0, high, extra)
        extra = jnp.where(at == 1, middle, extra)
        extra = jnp.where(at == 2, rest - middle, extra)
    block = jnp.concatenate([token, share, extra], axis=1).astype(bf16)
    block_ref[...] = jnp.broadcast_to(block[None], block_ref.shape)
    for fetch in fetches:
        fetch.wait()


def lay_half(far, rows_ref, start, put, i):
    far_y, far_z = far
    count = far_y * far_z
    pairs = count // 16
    near, two = i // 2, i % 2
    near_y, near_z = near // 2, near % 2
    for pair in range(pairs):

        def rows_of(chip):
            return pl.ds((chip * 4 + near) * count + pair * 16, 16)

        for b in range(8):
            lanes = slice(start + b * 128, start + (b + 1) * 128)
            low = rows_ref[rows_of(2 * two), lanes].astype(f32)
            high = rows_ref[rows_of(2 * two + 1), lanes].astype(f32)
            for half in range(2):
                place = 8 * (2 * pair + half) + b
                y, z = 2 * (place // far_z) + near_y, 2 * (place % far_z) + near_z
                part = slice(8 * half, 8 * half + 8)
                put(
                    y * 2 * far_z + z,
                    two,
                    jnp.concatenate([low[part], high[part]], axis=0).astype(bf16),
                )


def early_kernel(far, own_ref, mine_ref, other_ref, total, half_ref):
    both = mine_ref.shape[0] // 3 * 2
    width = mine_ref.shape[1]

    def put(line, two, rows):
        half_ref[pl.ds(32 * line + 16 * two, 16), :] = rows

    for i in range(8):
        lay_half(far, own_ref, width, put, i)
    for i, weights in enumerate([mine_ref, other_ref]):
        total[:, 512 * i : 512 * i + both] = contract(
            own_ref[:, :width], weights[:both, :]
        )


def late_kernel(
    far,
    place,
    own_ref,
    half_ref,
    came_ref,
    out_maps_ref,
    total,
    mine_ref,
    other_ref,
    sum_ref,
    maps_ref,
    down_ref,
):
    core = place[0]
    units = out_maps_ref.shape[0]
    rank = out_maps_ref.shape[1] // 2
    width = maps_ref.shape[0]

    def put(line, two, rows):
        at = 64 * line + 32 * (1 - core) + 16 * two
        maps_ref[pl.ds(pl.multiple_of(at, 16), 16), :] = rows

    def mine(line, carry):
        at = pl.ds(pl.multiple_of(64 * line + 32 * core, 32), 32)
        maps_ref[at, :] = half_ref[pl.ds(pl.multiple_of(32 * line, 32), 32), :]
        return carry

    lax.fori_loop(0, width // 64, mine, 0)
    for i in range(8):
        lay_half(far, came_ref, 0, put, i)
    low = matmul(own_ref[:, :width], maps_ref[...], False).astype(bf16)
    parts = own_ref[:, width + 1024 :].astype(f32)
    lane = lax.broadcasted_iota(jnp.int32, parts.shape, 1)
    hidden = []
    for i, (expert, out_maps, down) in enumerate(
        [
            (place[1], out_maps_ref[...], mine_ref),
            (place[1] + 1 - 2 * core, came_ref[:units, 1024:], other_ref),
        ]
    ):
        at = 512 * i
        gate = total[:, at : at + units] + adapter_scale * contract(
            low[:, :rank], out_maps[:, :rank]
        )
        up = total[:, at + units : at + 2 * units] + adapter_scale * contract(
            low[:, rank:], out_maps[:, rank:]
        )
        named = (lane >= 3 * expert) & (lane < 3 * expert + 3)
        weight = jnp.sum(jnp.where(named, parts, 0.0), axis=1, keepdims=True)
        hidden.append((jax.nn.silu(gate) * up * weight).astype(bf16))
        down_ref[units * i : units * (i + 1), :] = down[2 * units :, :]
    sum_ref[...] = matmul(
        jnp.concatenate(hidden, axis=1), down_ref[...], False
    ).astype(bf16)


def last_kernel(parts_ref, mixed_ref):
    whole = jnp.sum(parts_ref[...].astype(f32), axis=0)
    mixed_ref[...] = jnp.concatenate(
        [whole[s : s + 1, :] for s in range(8)], axis=1
    ).astype(bf16)


def on_device(
    tokens,
    routes,
    routing_weight,
    gate_weight,
    up_weight,
    down_weight,
    adapter_input_maps,
    adapter_output_maps,
):
    chips, cores = lax.axis_size("x"), lax.axis_size("core")
    far = (lax.axis_size("y_far"), lax.axis_size("z_far"))
    few = far[0] * far[1]
    groups = chips * 4
    core = lax.axis_index("core")
    expert = lax.axis_index("x") * cores + core
    width = tokens.shape[2]
    units = gate_weight.shape[1]
    piece = width // 8
    count = groups * few

    place = jnp.stack([core, expert]).astype(jnp.int32)
    blocks, weights = on_core(
        block_kernel,
        (((few, 8, piece + 256), bf16), ((3 * units, width), bf16)),
        (
            pltpu.SMEM(routes.shape[:0:-1], jnp.int32),
            pltpu.SMEM(routes.shape[:0:-1], f32),
            pltpu.VMEM((1, width), bf16),
            pltpu.VMEM(adapter_input_maps.shape, bf16),
            pltpu.VMEM(adapter_input_maps.shape, f32),
            pltpu.SemaphoreType.DMA((7,)),
        ),
        1,
        0,
        7,
    )(
        place,
        far_held(routes[0].T),
        far_held(routing_weight[0].T),
        far_held(tokens[0]),
        far_held(adapter_input_maps),
        far_held(gate_weight[0]),
        far_held(up_weight[0]),
        far_held(down_weight[0]),
    )
    swap = [(0, 1), (1, 0)]
    other_weights = lax.ppermute(weights, "core", swap)
    got = lax.all_to_all(blocks, FAR, 0, 0, tiled=True)
    got, other_weights = lax.optimization_barrier((got, other_weights))
    rows = got[:, :, :piece].reshape(few, width)
    maps_tiles = (
        got[:, :, piece : piece + 128]
        .reshape(few // 8, 8, 8, 128)
        .transpose(0, 2, 1, 3)
        .reshape(few, 1024)
    )
    packed = jnp.concatenate([rows, maps_tiles, got[:, 0, piece + 128 :]], axis=1)
    own = spread(packed, NEAR, groups).reshape(count, -1)

    out_maps = adapter_output_maps[0].T
    other = jnp.concatenate(
        [
            own[:, width : width + 1024],
            jnp.pad(out_maps, ((0, count - units), (0, 0))),
        ],
        axis=1,
    )
    came = lax.ppermute(other, "core", swap)
    own, weights, other_weights = held(own), held(weights), held(other_weights)
    base, half = on_core(
        functools.partial(early_kernel, far),
        (((count, 1024), f32), ((width // 2, 128), bf16)),
        (),
        0,
        3,
    )(own, weights, other_weights)
    (both,) = on_core(
        functools.partial(late_kernel, far),
        (((count, width), bf16),),
        (pltpu.VMEM((width, 128), bf16), pltpu.VMEM((2 * units, width), bf16)),
        1,
        7,
    )(
        place,
        own,
        held(half),
        held(came),
        held(out_maps),
        held(base),
        weights,
        other_weights,
    )
    near = lax.all_to_all(both, NEAR, 0, 0, tiled=True).reshape(groups, few, width)
    column = jnp.sum(near.astype(f32), axis=0).astype(bf16)
    whole = lax.all_to_all(column.reshape(few, 8, piece), FAR, 0, 0, tiled=True)
    (mixed,) = on_core(last_kernel, (((1, width), bf16),), (), 0, 1)(held(whole))
    return mixed.reshape(1, 1, width)


def solution(mesh):
    expert, line = mesh.devices.shape
    fine = Mesh(
        mesh.devices.reshape(expert // 2, 2, line // 16, 2, 4, 2),
        ("x", "core") + LINE,
    )
    wide = ("x", "core")
    in_specs = (
        P(LINE, wide, None),
        P(LINE, None, None),
        P(LINE, None, None),
        P(wide, LINE, None),
        P(wide, LINE, None),
        P(wide, LINE, None),
        P(LINE, None),
        P(wide, None, LINE),
    )
    return jax.shard_map(
        on_device, mesh=fine, in_specs=in_specs, out_specs=P(LINE, wide, None), check_vma=False
    )
```
